32 devices in a mesh: ctx: 2 (over y), head: 4 (over x, core), resp: 4 (over z).
Axes of the slice: x: 2, y: 2, z: 4, core: 2. Of those that a mesh axis runs over, the one named last changes fastest.
Arguments:
- prompt_query: bfloat16 [2048, 64, 128], P(('ctx', 'head'), 'resp'), may hold values from -6 to 6
- prompt_key: bfloat16 [2048, 64, 128], P(('ctx', 'head'), 'resp'), may hold values from -6 to 6
- prompt_value: bfloat16 [2048, 64, 128], P(('ctx', 'head'), 'resp'), may hold values from -6 to 6
- prompt_cotangent: bfloat16 [2048, 64, 128], P(('ctx', 'head'), 'resp'), may hold values from -6 to 6
- reply_query: bfloat16 [4, 512, 64, 128], P('resp', None, ('ctx', 'head')), may hold values from -6 to 6
- reply_key: bfloat16 [4, 512, 64, 128], P('resp', None, ('ctx', 'head')), may hold values from -6 to 6
- reply_value: bfloat16 [4, 512, 64, 128], P('resp', None, ('ctx', 'head')), may hold values from -6 to 6
- reply_cotangent: bfloat16 [4, 512, 64, 128], P('resp', None, ('ctx', 'head')), may hold values from -6 to 6
- reply_weight: float32 [4], P('resp'), may hold values from 0.5 to 2
- reply_length: int32 [4], P('resp'), may hold values from 1 to 512, 1536 in all
Outputs:
- prompt_output: bfloat16 [2048, 64, 128], P(('ctx', 'head'), 'resp')
- reply_output: bfloat16 [4, 512, 64, 128], P('resp', None, ('ctx', 'head'))
- prompt_query_grad: bfloat16 [2048, 64, 128], P(('ctx', 'head'), 'resp')
- prompt_key_grad: bfloat16 [2048, 64, 128], P(('ctx', 'head'), 'resp')
- prompt_value_grad: bfloat16 [2048, 64, 128], P(('ctx', 'head'), 'resp')
- reply_query_grad: bfloat16 [4, 512, 64, 128], P('resp', None, ('ctx', 'head'))
- reply_key_grad: bfloat16 [4, 512, 64, 128], P('resp', None, ('ctx', 'head'))
- reply_value_grad: bfloat16 [4, 512, 64, 128], P('resp', None, ('ctx', 'head'))
The draws below stay inside these ranges and needn't reach their ends.
Inputs may be any that keep to these rules, and one draw needn't show every extreme that they name: `reply_length`: the longest response has exactly 512 live tokens; the slots of a response from its length on are padding.
All inputs are finite; a program needn't handle non-finite values. No bound on the sum of `reply_length` on one device may be relied on, other than what follows from the above.
Results may differ from the reference program's by a relative error of at most 0.0095.
Values sent between devices are 32-bit elements; how exact they have to be, the bound alone decides.
No kernel may reach another device: no remote copies, remote signals or barrier semaphores. Data moves between devices by JAX's collectives and lax.ppermute only.
A program may use at most 128 MiB of HBM per device.

```python
import math
import jax
import jax.numpy as jnp
import numpy as np
from jax import lax

H = 64
E = 128
PROMPT_DEV = 256
L = 512
R = 4
P_SIZE = 2048


def level_of(stream_key, shape, split, low, high):
    factor_of, own = 1.0, jax.random.fold_in(stream_key, 6)
    for axis_at, parts in split:
        draws = jnp.exp(jax.random.uniform(jax.random.fold_in(own, axis_at), (parts,), jnp.float32, low / len(split), high / len(split)))
        factor_of = factor_of * jnp.repeat(draws, shape[axis_at] // parts).reshape([-1 if axis == axis_at else 1 for axis in range(len(shape))])
    return factor_of


def length_profile(count, total, reach, lean):
    portions = [(1 << 20) // math.isqrt(rank ** lean) + 1 for rank in range(2, count + 1)]
    spare, holding = total - reach - (count - 1), [1] * (count - 1)
    while spare > 0:
        candidates = [i for i in range(count - 1) if holding[i] < reach]
        whole, budget = sum([portions[i] for i in candidates]), spare
        for i in candidates:
            more = min(reach - holding[i], max(1, budget * portions[i] // whole), spare)
            holding[i] = holding[i] + more
            spare = spare - more
    return np.array([reach] + holding)


def ragged_sizes(stream_key, number_of, total, limit, lean):
    if number_of == 2:
        one = jax.random.randint(stream_key, (), max(1, total - limit), min(limit, total - 1) + 1)
        return jnp.stack([one, total - one])
    lengths = jnp.asarray(length_profile(number_of, total, limit, lean), jnp.int32)
    couples = (number_of - 1) // 2
    source_of, taker = lengths[1:1 + 2 * couples:2], lengths[2:2 + 2 * couples:2]
    room = jnp.minimum(source_of - 1, limit - taker)
    shifted = jax.random.randint(jax.random.fold_in(stream_key, 1), (couples,), 0, 1 << 20) % (room + 1)
    lengths = lengths.at[1:1 + 2 * couples:2].set(source_of - shifted).at[2:2 + 2 * couples:2].set(taker + shifted)
    return lengths[jax.random.permutation(jax.random.fold_in(stream_key, 2), number_of)]


def centred(own_key, extent, width, most, cuts=(), kind=jnp.bfloat16):
    factor_of = level_of(own_key, extent, cuts, -0.22, 0.18) if cuts else 1.0
    result = jax.random.normal(own_key, extent, jnp.float32) * width * factor_of
    return jnp.minimum(jnp.maximum(result, -most), most).astype(kind)


def setup_inputs(seed: int = 0) -> dict:
    seeds = jax.random.split(jax.random.key(seed), 11)
    return {
        "prompt_query": centred(seeds[0], (P_SIZE, H, E), 1.0, 6.0, ((0, 8), (1, 4))),
        "prompt_key": centred(seeds[1], (P_SIZE, H, E), 1.0, 6.0, ((0, 8), (1, 4))),
        "prompt_value": centred(seeds[2], (P_SIZE, H, E), 1.0, 6.0, ((0, 8), (1, 4))),
        "prompt_cotangent": centred(seeds[3], (P_SIZE, H, E), 1.0, 6.0, ((0, 8), (1, 4))),
        "reply_query": centred(seeds[4], (R, L, H, E), 1.0, 6.0, ((0, 4), (2, 8))),
        "reply_key": centred(seeds[5], (R, L, H, E), 1.0, 6.0, ((0, 4), (2, 8))),
        "reply_value": centred(seeds[6], (R, L, H, E), 1.0, 6.0, ((0, 4), (2, 8))),
        "reply_cotangent": centred(seeds[7], (R, L, H, E), 1.0, 6.0, ((0, 4), (2, 8))),
        "reply_weight": jnp.clip(0.5 + 1.5 * jax.random.uniform(seeds[8], (R,), jnp.float32) ** level_of(seeds[8], (R,), ((0, 4),), -0.2, 0.2), 0.5, 2.0),
        "reply_length": ragged_sizes(seeds[9], R, R * L * 3 // 4, L, 1).astype(jnp.int32),
    }


def position_scale(first_row, row_total):
    positions = (first_row + jnp.arange(row_total, dtype=jnp.int32)).astype(jnp.float32)
    return lax.rsqrt(E * (positions + 1.0))

def causal_mask(row_total):
    return jnp.arange(row_total)[:, None] >= jnp.arange(row_total)[None, :]

def forward_pieces(query, key_rows, value_rows, row_scale):
    causal = causal_mask(query.shape[0])
    scores = jnp.einsum('thd,shd->hts', query.astype(jnp.float32), key_rows.astype(jnp.float32), precision=lax.Precision.HIGHEST)
    mixing = jnp.where(causal[None], scores * row_scale[None, :, None], 0.0).astype(jnp.bfloat16)
    inner_sum = jnp.einsum('hts,she->the', mixing.astype(jnp.float32), value_rows.astype(jnp.float32), precision=lax.Precision.HIGHEST)
    return (mixing, inner_sum)

def carried_term(query, state_in, row_scale):
    product = jnp.einsum('thd,hde->the', query.astype(jnp.float32), state_in, precision=lax.Precision.HIGHEST)
    return row_scale[:, None, None] * product

def local_state(key_rows, value_rows):
    return jnp.einsum('shd,she->hde', key_rows.astype(jnp.float32), value_rows.astype(jnp.float32), precision=lax.Precision.HIGHEST)

def local_moment(query, cotangent, row_scale):
    scaled = query.astype(jnp.float32) * row_scale[:, None, None]
    return jnp.einsum('thd,the->hde', scaled, cotangent.astype(jnp.float32), precision=lax.Precision.HIGHEST)

def backward_pieces(query, key_rows, value_rows, cotangent, mixing, row_scale, state_in, suffix_in):
    causal = causal_mask(query.shape[0])
    cot_wide = cotangent.astype(jnp.float32)
    grad_mixing = jnp.einsum('the,she->hts', cot_wide, value_rows.astype(jnp.float32), precision=lax.Precision.HIGHEST)
    grad_scores = jnp.where(causal[None], grad_mixing * row_scale[None, :, None], 0.0).astype(jnp.bfloat16)
    grad_wide = grad_scores.astype(jnp.float32)
    grad_query = jnp.einsum('hts,shd->thd', grad_wide, key_rows.astype(jnp.float32), precision=lax.Precision.HIGHEST)
    grad_query = grad_query + row_scale[:, None, None] * jnp.einsum('the,hde->thd', cot_wide, state_in, precision=lax.Precision.HIGHEST)
    grad_key = jnp.einsum('hts,thd->shd', grad_wide, query.astype(jnp.float32), precision=lax.Precision.HIGHEST)
    grad_value = jnp.einsum('hts,the->she', mixing.astype(jnp.float32), cot_wide, precision=lax.Precision.HIGHEST)
    if suffix_in is not None:
        grad_key = grad_key + jnp.einsum('she,hde->shd', value_rows.astype(jnp.float32), suffix_in, precision=lax.Precision.HIGHEST)
        grad_value = grad_value + jnp.einsum('shd,hde->she', key_rows.astype(jnp.float32), suffix_in, precision=lax.Precision.HIGHEST)
    return (grad_query.astype(jnp.bfloat16), grad_key.astype(jnp.bfloat16), grad_value.astype(jnp.bfloat16))

def reference(prompt_query, prompt_key, prompt_value, prompt_cotangent, reply_query, reply_key, reply_value, reply_cotangent, reply_weight, reply_length):
    blocks = P_SIZE // PROMPT_DEV

    def split_blocks(array):
        return array.reshape(blocks, PROMPT_DEV, H, E)
    prompt_inputs = (split_blocks(prompt_query), split_blocks(prompt_key), split_blocks(prompt_value), split_blocks(prompt_cotangent), jnp.arange(blocks, dtype=jnp.int32))

    def prompt_forward(running, inputs):
        query, key_rows, value_rows, cotangent, block_number = inputs
        row_scale = position_scale(block_number * PROMPT_DEV, PROMPT_DEV)
        mixing, inner_sum = forward_pieces(query, key_rows, value_rows, row_scale)
        output = inner_sum + carried_term(query, running, row_scale)
        return (running + local_state(key_rows, value_rows), (output.astype(jnp.bfloat16), running))
    zero_state = jnp.zeros((H, E, E), jnp.float32)
    final_state, (prompt_blocks, before_states) = lax.scan(prompt_forward, zero_state, prompt_inputs)
    reply_scale = position_scale(P_SIZE, L)

    def reply_pass(running, inputs):
        query, key_rows, value_rows, cotangent, weight_value, length_value = inputs
        live_mask = (jnp.arange(L, dtype=jnp.int32) < length_value)[:, None, None]
        mixing, inner_sum = forward_pieces(query, key_rows, value_rows, reply_scale)
        output = jnp.where(live_mask, inner_sum + carried_term(query, final_state, reply_scale), 0.0).astype(jnp.bfloat16)
        weighted = (weight_value * jnp.where(live_mask, cotangent.astype(jnp.float32), 0.0)).astype(jnp.bfloat16)
        grads = backward_pieces(query, key_rows, value_rows, weighted, mixing, reply_scale, final_state, None)
        return (running + local_moment(query, weighted, reply_scale), (output,) + grads)
    reply_moment, reply_results = lax.scan(reply_pass, zero_state, (reply_query, reply_key, reply_value, reply_cotangent, reply_weight, reply_length))

    def prompt_backward(running, inputs):
        query, key_rows, value_rows, cotangent, block_number, state_in = inputs
        row_scale = position_scale(block_number * PROMPT_DEV, PROMPT_DEV)
        mixing, inner_sum = forward_pieces(query, key_rows, value_rows, row_scale)
        grads = backward_pieces(query, key_rows, value_rows, cotangent, mixing, row_scale, state_in, running)
        return (running + local_moment(query, cotangent, row_scale), grads)
    spent_moment, prompt_grads = lax.scan(prompt_backward, reply_moment, prompt_inputs + (before_states,), reverse=True)

    def join_blocks(array):
        return array.reshape(P_SIZE, H, E)
    return (join_blocks(prompt_blocks), reply_results[0], join_blocks(prompt_grads[0]), join_blocks(prompt_grads[1]), join_blocks(prompt_grads[2]), reply_results[1], reply_results[2], reply_results[3])
```

```python
import jax
import jax.numpy as jnp
from jax import lax
from jax.sharding import PartitionSpec as P

PLANE = ("ctx", "head")


def pair_step(block):
    count = lax.axis_size(PLANE)
    return lax.ppermute(block, PLANE, [(b, b ^ 1) for b in range(count)])


def plane_exchange(pieces):
    count = lax.axis_size(PLANE)
    moved = [pieces[0]]
    for k in range(1, len(pieces)):
        moved.append(lax.ppermute(pieces[k], PLANE, [(b, b ^ (2 * k)) for b in range(count)]))
    return moved


def resp_exchange(pieces):
    count = lax.axis_size("resp")
    moved = [pieces[0]]
    for k in range(1, len(pieces)):
        moved.append(lax.ppermute(pieces[k], "resp", [(z, z ^ k) for z in range(count)]))
    return moved


def choose(pieces, place):
    chosen = pieces[0]
    for k in range(1, len(pieces)):
        chosen = jnp.where(place == k, pieces[k], chosen)
    return chosen


def masked_sum(pieces, keep):
    total = None
    for piece, kept in zip(pieces, keep):
        term = jnp.where(kept, piece, 0.0)
        total = term if total is None else total + term
    return total


def joined(pieces, place):
    return jnp.concatenate([choose(pieces, place ^ q) for q in range(len(pieces))], 0)


def both_halves(half, member):
    other = pair_step(half)
    return jnp.concatenate(
        [jnp.where(member == 0, half, other), jnp.where(member == 0, other, half)], 0
    )


def position_scale(first_row, row_total, head_size):
    positions = (first_row + jnp.arange(row_total, dtype=jnp.int32)).astype(jnp.float32)
    return lax.rsqrt(float(head_size) * (positions + 1.0))


def causal_mask(row_total):
    return jnp.arange(row_total)[:, None] >= jnp.arange(row_total)[None, :]


def split_wide(wide):
    upper = wide.astype(jnp.bfloat16)
    lower = (wide - upper.astype(jnp.float32)).astype(jnp.bfloat16)
    return (upper, lower)


def narrow_first(form, narrow, wide):
    upper, lower = split_wide(wide)
    first = jnp.einsum(form, narrow, upper, preferred_element_type=jnp.float32)
    return first + jnp.einsum(form, narrow, lower, preferred_element_type=jnp.float32)


def wide_first(form, wide, narrow):
    upper, lower = split_wide(wide)
    first = jnp.einsum(form, upper, narrow, preferred_element_type=jnp.float32)
    return first + jnp.einsum(form, lower, narrow, preferred_element_type=jnp.float32)


def forward_pieces(query, key_rows, value_rows, row_scale):
    causal = causal_mask(query.shape[0])
    scores = jnp.einsum("thd,shd->hts", query, key_rows, preferred_element_type=jnp.float32)
    mixing = jnp.where(causal[None], scores * row_scale[None, :, None], 0.0).astype(jnp.bfloat16)
    inner_sum = jnp.einsum("hts,she->the", mixing, value_rows, preferred_element_type=jnp.float32)
    return (mixing, inner_sum)


def carried_term(query, state_in, row_scale):
    product = narrow_first("thd,hde->the", query, state_in)
    return row_scale[:, None, None] * product


def local_state(key_rows, value_rows):
    return jnp.einsum("shd,she->hde", key_rows, value_rows, preferred_element_type=jnp.float32)


def local_moment(query, cotangent, row_scale):
    scaled = query.astype(jnp.float32) * row_scale[:, None, None]
    return wide_first("thd,the->hde", scaled, cotangent)


def backward_pieces(query, key_rows, value_rows, cotangent, mixing, row_scale, state_in, suffix_in):
    causal = causal_mask(query.shape[0])
    grad_mixing = jnp.einsum(
        "the,she->hts", cotangent, value_rows, preferred_element_type=jnp.float32
    )
    grad_scores = jnp.where(causal[None], grad_mixing * row_scale[None, :, None], 0.0).astype(
        jnp.bfloat16
    )
    grad_query = jnp.einsum(
        "hts,shd->thd", grad_scores, key_rows, preferred_element_type=jnp.float32
    )
    grad_query = grad_query + row_scale[:, None, None] * narrow_first(
        "the,hde->thd", cotangent, state_in
    )
    grad_key = jnp.einsum("hts,thd->shd", grad_scores, query, preferred_element_type=jnp.float32)
    grad_value = jnp.einsum("hts,the->she", mixing, cotangent, preferred_element_type=jnp.float32)
    if suffix_in is not None:
        grad_key = grad_key + narrow_first("she,hde->shd", value_rows, suffix_in)
        grad_value = grad_value + narrow_first("shd,hde->she", key_rows, suffix_in)
    return (
        grad_query.astype(jnp.bfloat16),
        grad_key.astype(jnp.bfloat16),
        grad_value.astype(jnp.bfloat16),
    )


def shards(
    prompt_query,
    prompt_key,
    prompt_value,
    prompt_cotangent,
    reply_query,
    reply_key,
    reply_value,
    reply_cotangent,
    reply_weight,
    reply_length,
):
    prompt_rows = prompt_query.shape[0]
    prompt_heads = prompt_query.shape[1]
    head_size = prompt_query.shape[2]
    reply_rows = reply_query.shape[1]
    reply_heads = reply_query.shape[2]
    block_count = lax.axis_size(PLANE)
    resp_count = lax.axis_size("resp")
    assert block_count == 2 * resp_count and resp_count & (resp_count - 1) == 0
    block_index = lax.axis_index(PLANE)
    resp_index = lax.axis_index("resp")
    pair_index, member = block_index // 2, block_index % 2
    state_rows = prompt_heads * head_size
    half_rows = state_rows // 2
    chunk_rows = half_rows // resp_count
    steps = range(resp_count)
    prompt_scale = position_scale(block_index * prompt_rows, prompt_rows, head_size)
    reply_scale = position_scale(block_count * prompt_rows, reply_rows, head_size)
    query_rows = reply_query[0]
    key_rows = reply_key[0]
    value_rows = reply_value[0]
    live_mask = (jnp.arange(reply_rows, dtype=jnp.int32) < reply_length[0])[:, None, None]
    weighted = (
        reply_weight[0] * jnp.where(live_mask, reply_cotangent[0].astype(jnp.float32), 0.0)
    ).astype(jnp.bfloat16)

    def scattered(mine, other):
        pair_sum = mine + other
        pieces = [
            lax.dynamic_slice_in_dim(
                pair_sum, member * half_rows + (pair_index ^ k) * chunk_rows, chunk_rows, 0
            )
            for k in steps
        ]
        return plane_exchange(pieces)

    reply_local = local_moment(query_rows, weighted, reply_scale).reshape(half_rows, head_size)
    reply_parts = plane_exchange(
        [
            lax.dynamic_slice_in_dim(reply_local, (pair_index ^ k) * chunk_rows, chunk_rows, 0)
            for k in steps
        ]
    )
    prompt_local = local_state(prompt_key, prompt_value).reshape(state_rows, head_size)
    other_local = pair_step(prompt_local)
    state_parts = scattered(prompt_local, other_local)
    moment_local = local_moment(prompt_query, prompt_cotangent, prompt_scale)
    moment_local = moment_local.reshape(state_rows, head_size)
    other_moment = pair_step(moment_local)
    moment_parts = scattered(moment_local, other_moment)

    final_chunk = masked_sum(state_parts, [True] * resp_count)
    final_parts = resp_exchange([final_chunk] * resp_count)
    reply_state = joined(
        plane_exchange([choose(final_parts, resp_index ^ pair_index ^ k) for k in steps]),
        pair_index,
    ).reshape(reply_heads, head_size, head_size)

    before_half = joined(
        plane_exchange(
            [
                masked_sum(state_parts, [(pair_index ^ m) < (pair_index ^ k) for m in steps])
                for k in steps
            ]
        ),
        pair_index,
    )
    prompt_before = both_halves(before_half, member) + jnp.where(member == 1, other_local, 0.0)
    prompt_before = prompt_before.reshape(prompt_heads, head_size, head_size)

    reply_chunk = masked_sum(
        resp_exchange([choose(reply_parts, resp_index ^ pair_index ^ j) for j in steps]),
        [True] * resp_count,
    )
    after_half = joined(
        plane_exchange(
            [
                reply_chunk
                + masked_sum(moment_parts, [(pair_index ^ m) > (pair_index ^ k) for m in steps])
                for k in steps
            ]
        ),
        pair_index,
    )
    suffix = both_halves(after_half, member) + jnp.where(member == 0, other_moment, 0.0)
    suffix = suffix.reshape(prompt_heads, head_size, head_size)

    prompt_mixing, prompt_inner = forward_pieces(
        prompt_query, prompt_key, prompt_value, prompt_scale
    )
    prompt_output = (prompt_inner + carried_term(prompt_query, prompt_before, prompt_scale)).astype(
        jnp.bfloat16
    )
    reply_mixing, reply_inner = forward_pieces(query_rows, key_rows, value_rows, reply_scale)
    reply_output = jnp.where(
        live_mask, reply_inner + carried_term(query_rows, reply_state, reply_scale), 0.0
    ).astype(jnp.bfloat16)
    reply_dquery, reply_dkey, reply_dvalue = backward_pieces(
        query_rows, key_rows, value_rows, weighted, reply_mixing, reply_scale, reply_state, None
    )
    prompt_dquery, prompt_dkey, prompt_dvalue = backward_pieces(
        prompt_query,
        prompt_key,
        prompt_value,
        prompt_cotangent,
        prompt_mixing,
        prompt_scale,
        prompt_before,
        suffix,
    )
    return (
        prompt_output,
        reply_output[None],
        prompt_dquery,
        prompt_dkey,
        prompt_dvalue,
        reply_dquery[None],
        reply_dkey[None],
        reply_dvalue[None],
    )


def solution(mesh):
    placed = (
        P(("ctx", "head"), "resp", None),
        P(("ctx", "head"), "resp", None),
        P(("ctx", "head"), "resp", None),
        P(("ctx", "head"), "resp", None),
        P("resp", None, ("ctx", "head"), None),
        P("resp", None, ("ctx", "head"), None),
        P("resp", None, ("ctx", "head"), None),
        P("resp", None, ("ctx", "head"), None),
        P("resp"),
        P("resp"),
    )
    return jax.shard_map(
        shards,
        mesh=mesh,
        in_specs=placed,
        out_specs=(
            P(("ctx", "head"), "resp", None),
            P("resp", None, ("ctx", "head"), None),
            P(("ctx", "head"), "resp", None),
            P(("ctx", "head"), "resp", None),
            P(("ctx", "head"), "resp", None),
            P("resp", None, ("ctx", "head"), None),
            P("resp", None, ("ctx", "head"), None),
            P("resp", None, ("ctx", "head"), None),
        ),
        check_vma=False,
    )
```

```python
import functools

import jax
import jax.numpy as jnp
from jax import lax
from jax.experimental import pallas as pl
from jax.experimental.pallas import tpu as pltpu
from jax.sharding import PartitionSpec as P

PLANE = ("ctx", "head")
BLOCK = 256
F32 = jnp.float32
BF16 = jnp.bfloat16
ROWS_ROWS = (((0,), (0,)), ((), ()))
LAST_LAST = (((1,), (1,)), ((), ()))
LAST_ROWS = (((1,), (0,)), ((), ()))


def pair_step(block):
    count = lax.axis_size(PLANE)
    return lax.ppermute(block, PLANE, [(b, b ^ 1) for b in range(count)])


def plane_exchange(pieces):
    count = lax.axis_size(PLANE)
    moved = [pieces[0]]
    for k in range(1, len(pieces)):
        moved.append(lax.ppermute(pieces[k], PLANE, [(b, b ^ (2 * k)) for b in range(count)]))
    return moved


def resp_exchange(pieces):
    count = lax.axis_size("resp")
    moved = [pieces[0]]
    for k in range(1, len(pieces)):
        moved.append(lax.ppermute(pieces[k], "resp", [(z, z ^ k) for z in range(count)]))
    return moved


def dot(a, b, dims):
    return lax.dot_general(a, b, dims, preferred_element_type=F32)


def row_scale(first_row, row_total, head_size):
    rows = lax.broadcasted_iota(jnp.int32, (row_total, head_size), 0) + first_row
    return lax.rsqrt(float(head_size) * (rows.astype(F32) + 1.0))


def by_head(array):
    return jnp.swapaxes(array, 0, 1)


def weighted_by_head(cotangent, weight, length):
    rows = lax.broadcasted_iota(jnp.int32, cotangent.shape, 1)
    return (weight * jnp.where(rows < length, cotangent.astype(F32), 0.0)).astype(BF16)


def load(sources, buffers, arrived):
    copies = []
    for i, (source, buffer) in enumerate(zip(sources, buffers)):
        copies.append(pltpu.make_async_copy(source, buffer, arrived.at[i]))
        copies[-1].start()
    return copies


def moments_kernel(steps, place, weight, *refs):
    sources, refs = refs[:6], refs[6:]
    sent, kept, key, value, query, cotangent, r_query, r_cotangent = refs[:8]
    pieces, refs = refs[8 : 8 + steps], refs[8 + steps :]
    buffers, (r_moment, arrived) = refs[:6], refs[6:]
    copies = load(sources, buffers, arrived)
    member, pair, first_row, reply_first, length = (place[i] for i in range(5))
    heads, rows, size = query.shape
    half = heads // 2
    halves = ((sent, (1 - member) * half), (kept, member * half))
    for i, target in enumerate((key, value)):
        copies[i].wait()
        target[...] = by_head(buffers[i][...])
    for target, base in halves:

        def state(j, carry, target=target, base=base):
            h = base + j
            target[pl.ds(j * size, size), :] = dot(key[h], value[h], ROWS_ROWS)
            return carry

        lax.fori_loop(0, half, state, 0, unroll=True)
    for i, target in enumerate((query, cotangent)):
        copies[2 + i].wait()
        target[...] = by_head(buffers[2 + i][...])
    scale = row_scale(first_row, rows, size)
    for target, base in halves:

        def moment(j, carry, target=target, base=base):
            h = base + j
            scaled = (query[h].astype(F32) * scale).astype(BF16)
            target[pl.ds((half + j) * size, size), :] = dot(scaled, cotangent[h], ROWS_ROWS)
            return carry

        lax.fori_loop(0, half, moment, 0, unroll=True)
    copies[4].wait()
    r_query[...] = by_head(buffers[4][...])
    copies[5].wait()
    r_cotangent[...] = weighted_by_head(by_head(buffers[5][...]), weight[0], length)
    scale = row_scale(reply_first, r_query.shape[1], size)
    for h in range(r_query.shape[0]):
        scaled = (r_query[h].astype(F32) * scale).astype(BF16)
        r_moment[pl.ds(h * size, size), :] = dot(scaled, r_cotangent[h], ROWS_ROWS)
    piece_rows = pieces[0].shape[0]
    for k in range(steps):
        start = pl.multiple_of((pair ^ k) * piece_rows, piece_rows)
        pieces[k][...] = r_moment[pl.ds(start, piece_rows), :]


def pair_kernel(steps, place, kept, received, *pieces):
    pair = place[1]
    half_rows = kept.shape[0] // 2
    piece_rows = half_rows // steps
    for k in range(steps):
        start = pl.multiple_of((pair ^ k) * piece_rows, piece_rows)
        for part in range(2):
            source = pl.ds(part * half_rows + start, piece_rows)
            pieces[k][pl.ds(part * piece_rows, piece_rows), :] = kept[source, :] + received[source, :]


def choose_kernel(steps, place, follows, *refs):
    pieces, outs = refs[:steps], refs[steps:]
    start = place[1] ^ place[5]
    for j in range(steps):
        chosen = pieces[0][...]
        for k in range(1, steps):
            chosen = jnp.where((start ^ j) == k, pieces[k][...], chosen)
        outs[j][...] = chosen


def prefix_kernel(steps, place, follows, *refs):
    parts, moments, refs = refs[:steps], refs[steps : 2 * steps], refs[2 * steps :]
    final, returned = refs[0], refs[1:]
    pair = place[1]
    rows = final.shape[0]
    states = [part[pl.ds(0, rows), :] for part in parts]
    total = states[0]
    for k in range(1, steps):
        total = total + states[k]
    final[...] = total
    for k in range(steps):
        before = jnp.zeros_like(total)
        for m in range(steps):
            before = before + jnp.where((pair ^ m) < (pair ^ k), states[m], 0.0)
        returned[k][pl.ds(0, rows), :] = before
    reply_moment = moments[0][...]
    for k in range(1, steps):
        reply_moment = reply_moment + moments[k][...]
    later = [part[pl.ds(rows, rows), :] for part in parts]
    for k in range(steps):
        after = reply_moment
        for m in range(steps):
            after = after + jnp.where((pair ^ m) > (pair ^ k), later[m], 0.0)
        returned[k][pl.ds(rows, rows), :] = after


def halves_kernel(steps, place, follows, kept, received, *refs):
    pieces, mine, to_other = refs[:steps], refs[steps], refs[steps + 1]
    member, pair = place[0], place[1]
    half_rows = kept.shape[0] // 2
    piece_rows = half_rows // steps
    first = member == 0
    for k in range(steps):
        start = pl.multiple_of((pair ^ k) * piece_rows, piece_rows)
        for part in range(2):
            rows = pl.ds(part * half_rows + start, piece_rows)
            sums = pieces[k][pl.ds(part * piece_rows, piece_rows), :]
            add_other = first if part else jnp.logical_not(first)
            mine[rows, :] = sums + jnp.where(add_other, received[rows, :], 0.0)
            to_other[rows, :] = sums + jnp.where(add_other, 0.0, kept[rows, :])


def prompt_local_kernel(
    place,
    query,
    key,
    value,
    cotangent,
    reply_key,
    reply_value,
    follows,
    inner,
    query_part,
    key_part,
    value_part,
    r_key,
    r_value,
    mask,
    key_buffer,
    value_buffer,
    arrived,
):
    heads, rows, size = query.shape
    copies = load((reply_key, reply_value), (key_buffer, value_buffer), arrived)
    mask[...] = causal_weights(place[2], rows, size)

    def one(h, carry):
        mixing = (dot(query[h], key[h], LAST_LAST) * mask[...]).astype(BF16)
        grad_mixing = (dot(cotangent[h], value[h], LAST_LAST) * mask[...]).astype(BF16)
        inner[h] = dot(mixing, value[h], LAST_ROWS)
        query_part[h] = dot(grad_mixing, key[h], LAST_ROWS)
        key_part[h] = dot(grad_mixing, query[h], ROWS_ROWS)
        value_part[h] = dot(mixing, cotangent[h], ROWS_ROWS)
        return carry

    lax.fori_loop(0, heads, one, 0, unroll=4)
    copies[0].wait()
    r_key[...] = by_head(key_buffer[...])
    copies[1].wait()
    r_value[...] = by_head(value_buffer[...])


def causal_weights(first_row, row_total, head_size):
    rows = lax.broadcasted_iota(jnp.int32, (row_total, row_total), 0)
    columns = lax.broadcasted_iota(jnp.int32, (row_total, row_total), 1)
    scale = lax.rsqrt(float(head_size) * ((rows + first_row).astype(F32) + 1.0))
    return jnp.where(rows >= columns, scale, 0.0)


def reply_local(first_head, first_row, query, key, value, cotangent, outs, mask):
    inner, query_part, key_rows, value_rows = outs
    heads, rows, size = inner.shape
    block = mask.shape[1]
    count = rows // block
    for i in range(count):
        mask[i] = causal_weights(first_row + i * block, block, size)

    def one(own, carry):
        h = first_head + own
        key_sum, value_sum = [None] * count, [None] * count
        for i in range(count):
            mine = pl.ds(i * block, block)
            inner_sum, query_sum = None, None
            for j in range(i + 1):
                other = pl.ds(j * block, block)
                weights = mask[i] if i == j else mask[i][:, :1]
                mixing = (dot(query[h, mine], key[h, other], LAST_LAST) * weights).astype(BF16)
                grad_mixing = dot(cotangent[h, mine], value[h, other], LAST_LAST) * weights
                grad_mixing = grad_mixing.astype(BF16)
                terms = (
                    dot(mixing, value[h, other], LAST_ROWS),
                    dot(grad_mixing, key[h, other], LAST_ROWS),
                    dot(grad_mixing, query[h, mine], ROWS_ROWS),
                    dot(mixing, cotangent[h, mine], ROWS_ROWS),
                )
                inner_sum = terms[0] if j == 0 else inner_sum + terms[0]
                query_sum = terms[1] if j == 0 else query_sum + terms[1]
                key_sum[j] = terms[2] if i == j else key_sum[j] + terms[2]
                value_sum[j] = terms[3] if i == j else value_sum[j] + terms[3]
            inner[own, mine] = inner_sum
            query_part[own, mine] = query_sum
        for j in range(count):
            other = pl.ds(j * block, block)
            key_rows[own, other] = key_sum[j].astype(BF16)
            value_rows[own, other] = value_sum[j].astype(BF16)
        return carry

    lax.fori_loop(0, heads, one, 0, unroll=True)


def reply_first_kernel(place, query, key, value, cotangent, follows, *refs):
    reply_local(0, place[3], query, key, value, cotangent, refs[:4], refs[4])


def reply_second_kernel(
    place,
    query,
    key,
    value,
    cotangent,
    key_first,
    value_first,
    follows,
    inner,
    query_part,
    key_grad,
    value_grad,
    key_rows,
    value_rows,
    mask,
    staged,
    left,
):
    first_head = key_first.shape[0]
    outs = (inner, query_part, key_rows, value_rows)
    reply_local(first_head, place[3], query, key, value, cotangent, outs, mask)
    copies = []
    parts = ((key_first, key_rows, key_grad), (value_first, value_rows, value_grad))
    for i, (first, second, target) in enumerate(parts):
        staged[i] = by_head(jnp.concatenate([first[...], second[...]], 0))
        copies.append(pltpu.make_async_copy(staged.at[i], target, left.at[i]))
        copies[-1].start()
    for copy in copies:
        copy.wait()


def prompt_final_kernel(
    place,
    mine,
    other,
    inner,
    query_part,
    key_part,
    value_part,
    query,
    key,
    value,
    cotangent,
    output,
    query_grad,
    key_grad,
    value_grad,
    before,
    after,
    held,
    staged,
    left,
):
    member, first_row = place[0], place[2]
    heads, rows, size = query.shape
    half = heads // 2
    scale = row_scale(first_row, rows, size)

    def narrow(target, offset):
        for source, base in ((mine, member * half), (other, (1 - member) * half)):
            for j in range(half):
                target[base + j] = source[pl.ds((offset + j) * size, size), :].astype(BF16)

    def finish(i, target):
        staged[i] = by_head(held[...])
        copy = pltpu.make_async_copy(staged.at[i], target, left.at[i])
        copy.start()
        return copy

    narrow(before, 0)
    for h in range(heads):
        held[h] = (inner[h] + scale * dot(query[h], before[h], LAST_ROWS)).astype(BF16)
    copies = [finish(0, output)]
    for h in range(heads):
        part = scale * dot(cotangent[h], before[h], LAST_LAST)
        held[h] = (query_part[h] + part).astype(BF16)
    copies.append(finish(1, query_grad))
    narrow(after, half)
    for h in range(heads):
        held[h] = (key_part[h] + dot(value[h], after[h], LAST_LAST)).astype(BF16)
    copies.append(finish(2, key_grad))
    for h in range(heads):
        held[h] = (value_part[h] + dot(key[h], after[h], LAST_ROWS)).astype(BF16)
    copies.append(finish(3, value_grad))
    for copy in copies:
        copy.wait()


def reply_final_kernel(steps, place, follows, *refs):
    pieces, refs = refs[:steps], refs[steps:]
    inner, query_part, (query, cotangent, output, query_grad) = refs[:2], refs[2:4], refs[4:8]
    state, held, staged, left = refs[8:]
    half = inner[0].shape[0]
    pair, first_row, length = place[1], place[3], place[4]
    heads, rows, size = query.shape
    piece_rows = pieces[0].shape[0]
    for k in range(steps):
        start = pl.multiple_of((pair ^ k) * piece_rows, piece_rows)
        state[pl.ds(start, piece_rows), :] = pieces[k][...].astype(BF16)
    scale = row_scale(first_row, rows, size)
    live = lax.broadcasted_iota(jnp.int32, (rows, size), 0) < length
    copies = []

    def finish(i, target):
        staged[i] = by_head(held[...])
        copies.append(pltpu.make_async_copy(staged.at[i], target, left.at[i]))
        copies[-1].start()

    for h in range(heads):
        final = state[pl.ds(h * size, size), :]
        whole = inner[h // half][h % half] + scale * dot(query[h], final, LAST_ROWS)
        held[h] = jnp.where(live, whole, 0.0).astype(BF16)
    finish(0, output)
    for h in range(heads):
        final = state[pl.ds(h * size, size), :]
        part = scale * dot(cotangent[h], final, LAST_LAST)
        held[h] = (query_part[h // half][h % half] + part).astype(BF16)
    finish(1, query_grad)
    for copy in copies:
        copy.wait()


VMEM = pl.BlockSpec(memory_space=pltpu.VMEM)
HBM = pl.BlockSpec(memory_space=pltpu.HBM)
ANY = pl.BlockSpec(memory_space=pl.ANY)


def call(kernel, scalars, arrays, outs, scratch, flops, name):
    arrays = [
        (spec, pltpu.with_memory_space_constraint(array, pltpu.HBM) if spec is HBM else array)
        for spec, array in arrays
    ]
    return pl.pallas_call(
        kernel,
        out_shape=[out for _, out in outs],
        in_specs=[pl.BlockSpec(memory_space=pltpu.SMEM)] * len(scalars) + [s for s, _ in arrays],
        out_specs=[spec for spec, _ in outs],
        scratch_shapes=scratch,
        compiler_params=pltpu.CompilerParams(vmem_limit_bytes=24 << 20),
        cost_estimate=pl.CostEstimate(flops=1, bytes_accessed=1, transcendentals=0),
        name=name,
    )(*scalars, *[array for _, array in arrays])


def held_in(spec, arrays):
    return [(spec, array) for array in arrays]


def shards(
    prompt_query,
    prompt_key,
    prompt_value,
    prompt_cotangent,
    reply_query,
    reply_key,
    reply_value,
    reply_cotangent,
    reply_weight,
    reply_length,
):
    rows, heads, size = prompt_query.shape
    reply_query, reply_key = reply_query[0], reply_key[0]
    reply_value, reply_cotangent = reply_value[0], reply_cotangent[0]
    reply_rows, reply_heads = reply_query.shape[:2]
    block_count = lax.axis_size(PLANE)
    steps = lax.axis_size("resp")
    assert block_count == 2 * steps and steps & (steps - 1) == 0
    block_index = lax.axis_index(PLANE)
    resp_index = lax.axis_index("resp")
    pair_index, member = block_index // 2, block_index % 2
    half_rows = heads // 2 * size
    piece_rows = half_rows // steps
    laps = range(steps)
    place = jnp.stack(
        [
            member,
            pair_index,
            block_index * rows,
            block_count * rows,
            reply_length[0],
            resp_index,
        ]
    ).astype(jnp.int32)
    shape = jax.ShapeDtypeStruct
    prompt_bf16 = shape((rows, heads, size), BF16)
    reply_bf16 = shape((reply_rows, reply_heads, size), BF16)
    prompt_held = shape((heads, rows, size), BF16)
    reply_held = shape((reply_heads, reply_rows, size), BF16)
    prompt_wide = shape((heads, rows, size), F32)
    piece = shape((piece_rows, size), F32)
    two_pieces = shape((2 * piece_rows, size), F32)
    two_halves = shape((2 * half_rows, size), F32)
    state_flops = 2 * heads * rows * size * size
    reply_flops = 2 * reply_heads * reply_rows * size * size
    block = min(BLOCK, reply_rows)

    def scratch(held, count=None):
        return pltpu.VMEM(held.shape if count is None else (count, *held.shape), held.dtype)

    sent, kept, key, value, query, cotangent, r_query, r_cotangent, *moments = call(
        functools.partial(moments_kernel, steps),
        [place, reply_weight],
        held_in(
            HBM,
            [prompt_key, prompt_value, prompt_query, prompt_cotangent, reply_query, reply_cotangent],
        ),
        held_in(
            VMEM, [two_halves] * 2 + [prompt_held] * 4 + [reply_held] * 2 + [piece] * steps
        ),
        [scratch(prompt_bf16)] * 4
        + [scratch(reply_bf16)] * 2
        + [pltpu.VMEM((reply_heads * size, size), F32), pltpu.SemaphoreType.DMA((6,))],
        2 * state_flops + reply_flops,
        "moments",
    )
    received = pair_step(sent)
    moments = plane_exchange(moments)
    pieces = call(
        functools.partial(pair_kernel, steps),
        [place],
        held_in(VMEM, [kept, received]),
        held_in(VMEM, [two_pieces] * steps),
        [],
        half_rows * size * 2,
        "pair_sums",
    )
    parts = plane_exchange(pieces)
    *prompt_parts, r_key, r_value = call(
        prompt_local_kernel,
        [place],
        held_in(VMEM, [query, key, value, cotangent])
        + held_in(HBM, [reply_key, reply_value])
        + held_in(ANY, pieces[:1]),
        held_in(VMEM, [prompt_wide] * 4 + [reply_held] * 2),
        [
            pltpu.VMEM((rows, rows), F32),
            scratch(reply_bf16),
            scratch(reply_bf16),
            pltpu.SemaphoreType.DMA((2,)),
        ],
        6 * state_flops * rows // size,
        "prompt_local",
    )
    moments = call(
        functools.partial(choose_kernel, steps),
        [place],
        held_in(ANY, [r_value]) + held_in(VMEM, moments),
        held_in(VMEM, [piece] * steps),
        [],
        piece_rows * size * steps,
        "choose_moments",
    )
    half_heads = reply_heads // 2
    half_wide = shape((half_heads, reply_rows, size), F32)
    half_held = shape((half_heads, reply_rows, size), BF16)
    masks = pltpu.VMEM((reply_rows // block, block, block), F32)
    reply_arrays = held_in(VMEM, [r_query, r_key, r_value, r_cotangent])
    inner_first, part_first, key_first, value_first = call(
        reply_first_kernel,
        [place],
        reply_arrays + held_in(ANY, moments[:1]),
        held_in(VMEM, [half_wide] * 2 + [half_held] * 2),
        [masks],
        3 * reply_flops * reply_rows // size,
        "reply_first",
    )
    moments = resp_exchange(moments)
    final, *returned = call(
        functools.partial(prefix_kernel, steps),
        [place],
        held_in(ANY, [inner_first]) + held_in(VMEM, [*parts, *moments]),
        held_in(VMEM, [piece] + [two_pieces] * steps),
        [],
        piece_rows * size * steps * steps,
        "prefix_sums",
    )
    finals = resp_exchange([final] * steps)
    returned = plane_exchange(returned)
    inner_second, part_second, reply_dkey, reply_dvalue = call(
        reply_second_kernel,
        [place],
        reply_arrays + held_in(VMEM, [key_first, value_first]) + held_in(ANY, [final]),
        held_in(VMEM, [half_wide] * 2) + held_in(HBM, [reply_bf16] * 2),
        [scratch(half_held)] * 2
        + [masks, scratch(reply_bf16, 2), pltpu.SemaphoreType.DMA((2,))],
        3 * reply_flops * reply_rows // size,
        "reply_second",
    )
    finals = call(
        functools.partial(choose_kernel, steps),
        [place],
        held_in(ANY, [inner_second]) + held_in(VMEM, finals),
        held_in(VMEM, [piece] * steps),
        [],
        piece_rows * size * steps,
        "choose_states",
    )
    chosen = finals[:1]
    finals = plane_exchange(finals)
    mine, to_other = call(
        functools.partial(halves_kernel, steps),
        [place],
        held_in(ANY, chosen) + held_in(VMEM, [kept, received, *returned]),
        held_in(VMEM, [two_halves] * 2),
        [],
        half_rows * size * 4,
        "halves",
    )
    other = pair_step(to_other)
    prompt_output, prompt_dquery, prompt_dkey, prompt_dvalue = call(
        prompt_final_kernel,
        [place],
        held_in(VMEM, [mine, other, *prompt_parts, query, key, value, cotangent]),
        held_in(HBM, [prompt_bf16] * 4),
        [pltpu.VMEM((heads, size, size), BF16)] * 2
        + [scratch(prompt_held), scratch(prompt_bf16, 4), pltpu.SemaphoreType.DMA((4,))],
        4 * state_flops,
        "prompt_final",
    )
    reply_output, reply_dquery = call(
        functools.partial(reply_final_kernel, steps),
        [place],
        held_in(ANY, [prompt_output])
        + held_in(VMEM, [*finals, inner_first, inner_second, part_first, part_second])
        + held_in(VMEM, [r_query, r_cotangent]),
        held_in(HBM, [reply_bf16] * 2),
        [
            pltpu.VMEM((reply_heads * size, size), BF16),
            scratch(reply_held),
            scratch(reply_bf16, 2),
            pltpu.SemaphoreType.DMA((2,)),
        ],
        2 * reply_flops,
        "reply_final",
    )
    return (
        prompt_output,
        reply_output[None],
        prompt_dquery,
        prompt_dkey,
        prompt_dvalue,
        reply_dquery[None],
        reply_dkey[None],
        reply_dvalue[None],
    )


def solution(mesh):
    prompt = P(PLANE, "resp", None)
    reply = P("resp", None, PLANE, None)
    return jax.shard_map(
        shards,
        mesh=mesh,
        in_specs=(prompt,) * 4 + (reply,) * 4 + (P("resp"),) * 2,
        out_specs=(prompt, reply, prompt, prompt, prompt, reply, reply, reply),
        check_vma=False,
    )
```

```python
import functools

import jax
import jax.numpy as jnp
from jax import lax
from jax.experimental import pallas as pl
from jax.experimental.pallas import tpu as pltpu
from jax.sharding import PartitionSpec as P

PLANE = ("ctx", "head")
BLOCK = 256
CHUNK = 64
F32 = jnp.float32
BF16 = jnp.bfloat16
ROWS_ROWS = (((0,), (0,)), ((), ()))
LAST_LAST = (((1,), (1,)), ((), ()))
LAST_ROWS = (((1,), (0,)), ((), ()))


def pair_step(block):
    count = lax.axis_size(PLANE)
    return lax.ppermute(block, PLANE, [(b, b ^ 1) for b in range(count)])


def plane_exchange(pieces):
    count = lax.axis_size(PLANE)
    moved = [pieces[0]]
    for k in range(1, len(pieces)):
        moved.append(lax.ppermute(pieces[k], PLANE, [(b, b ^ (2 * k)) for b in range(count)]))
    return moved


def resp_masks(count):
    return [3 if mask == 2 else mask for mask in (1 << i for i in range(count.bit_length() - 1))]


def resp_step(array, mask):
    count = lax.axis_size("resp")
    return lax.ppermute(array, "resp", [(z, z ^ mask) for z in range(count)])


def resp_gather(piece):
    held = {0: piece}
    for mask in resp_masks(lax.axis_size("resp")):
        held.update({j ^ mask: resp_step(array, mask) for j, array in list(held.items())})
    return [held[j] for j in range(len(held))]


def halving_order(count):
    order = [0]
    for mask in reversed(resp_masks(count)):
        order = order + [j ^ mask for j in order]
    return order


def dot(a, b, dims):
    return lax.dot_general(a, b, dims, preferred_element_type=F32)


def row_scale(first_row, row_total, head_size):
    rows = lax.broadcasted_iota(jnp.int32, (row_total, head_size), 0) + first_row
    return lax.rsqrt(float(head_size) * (rows.astype(F32) + 1.0))


def to_heads(target, source, factor=None):
    rows = source.shape[0]
    chunk = CHUNK if rows % CHUNK == 0 else rows

    def one(i, carry):
        span = pl.ds(pl.multiple_of(i * chunk, chunk), chunk)
        part = jnp.swapaxes(source[span], 0, 1)
        if factor is not None:
            part = (part.astype(F32) * factor[span][None]).astype(BF16)
        target[:, span, :] = part
        return carry

    lax.fori_loop(0, rows // chunk, one, 0)


def by_head(array):
    return jnp.swapaxes(array, 0, 1)


def load(sources, buffers, arrived):
    copies = []
    for i, (source, buffer) in enumerate(zip(sources, buffers)):
        copies.append(pltpu.make_async_copy(source, buffer, arrived.at[i]))
        copies[-1].start()
    return copies


def moments_kernel(steps, place, weight, *refs):
    sources, refs = refs[:6], refs[6:]
    sent, kept, key, value, query, cotangent, r_query, r_cotangent = refs[:8]
    pieces, refs = refs[8 : 8 + steps], refs[8 + steps :]
    buffers, (scaled, r_scaled, r_moment, factor, arrived) = refs[:6], refs[6:]
    copies = load(sources, buffers, arrived)
    member, first_row, reply_first, length = (place[i] for i in (0, 2, 3, 4))
    heads, rows, size = query.shape
    half = heads // 2
    halves = ((sent, (1 - member) * half), (kept, member * half))
    for i, target in enumerate((key, value)):
        copies[i].wait()
        to_heads(target, buffers[i])
    for target, base in halves:

        def state(j, carry, target=target, base=base):
            h = base + j
            target[pl.ds(j * size, size), :] = dot(key[h], value[h], ROWS_ROWS)
            return carry

        lax.fori_loop(0, half, state, 0, unroll=True)
    for i, target in enumerate((query, cotangent)):
        copies[2 + i].wait()
        to_heads(target, buffers[2 + i])
    scale = row_scale(first_row, rows, size)
    for h in range(heads):
        scaled[h] = (query[h].astype(F32) * scale).astype(BF16)
    for target, base in halves:

        def moment(j, carry, target=target, base=base):
            h = base + j
            target[pl.ds((half + j) * size, size), :] = dot(scaled[h], cotangent[h], ROWS_ROWS)
            return carry

        lax.fori_loop(0, half, moment, 0, unroll=True)
    copies[4].wait()
    to_heads(r_query, buffers[4])
    copies[5].wait()
    live = lax.broadcasted_iota(jnp.int32, factor.shape, 0) < length
    factor[...] = jnp.where(live, weight[0], 0.0)
    to_heads(r_cotangent, buffers[5], factor)
    scale = row_scale(reply_first, r_query.shape[1], size)
    for h in range(r_query.shape[0]):
        r_scaled[h] = (r_query[h].astype(F32) * scale).astype(BF16)
    for h in range(r_query.shape[0]):
        r_moment[pl.ds(h * size, size), :] = dot(r_scaled[h], r_cotangent[h], ROWS_ROWS)
    piece_rows = pieces[0].shape[0]
    for k in range(steps):
        start = pl.multiple_of((place[1] ^ k) * piece_rows, piece_rows)
        pieces[k][...] = r_moment[pl.ds(start, piece_rows), :]


def pair_kernel(steps, place, kept, received, *pieces):
    pair = place[1]
    half_rows = kept.shape[0] // 2
    piece_rows = half_rows // steps
    for k in range(steps):
        start = pl.multiple_of((pair ^ k) * piece_rows, piece_rows)
        for part in range(2):
            source = pl.ds(part * half_rows + start, piece_rows)
            pieces[k][pl.ds(part * piece_rows, piece_rows), :] = kept[source, :] + received[source, :]


def choose(place, pieces, targets):
    start = place[1] ^ place[5]
    for j, (target, rows) in targets.items():
        chosen = pieces[0][...]
        for k in range(1, len(pieces)):
            chosen = jnp.where((start ^ j) == k, pieces[k][...], chosen)
        target[rows, :] = chosen


def choose_kernel(steps, place, follows, *refs):
    pieces, (stays, leaves, token) = refs[:steps], refs[steps:]
    token[...] = jnp.zeros_like(token)
    rows = pieces[0].shape[0]
    order, half = halving_order(steps), steps // 2
    targets = {
        j: (leaves if i >= half else stays, pl.ds(i % half * rows, rows)) for i, j in enumerate(order)
    }
    choose(place, pieces, targets)


def halve_kernel(follows, mine, other, stays, leaves):
    rows = stays.shape[0]
    stays[...] = mine[pl.ds(0, rows), :] + other[pl.ds(0, rows), :]
    leaves[...] = mine[pl.ds(rows, rows), :] + other[pl.ds(rows, rows), :]


def prefix_kernel(steps, place, follows, *refs):
    parts, moments, refs = refs[:steps], refs[steps : steps + 2], refs[steps + 2 :]
    final, returned = refs[0], refs[1:]
    pair = place[1]
    rows = final.shape[0]
    states = [part[pl.ds(0, rows), :] for part in parts]
    total = states[0]
    for k in range(1, steps):
        total = total + states[k]
    final[...] = total
    for k in range(steps):
        before = jnp.zeros_like(total)
        for m in range(steps):
            before = before + jnp.where((pair ^ m) < (pair ^ k), states[m], 0.0)
        returned[k][pl.ds(0, rows), :] = before
    reply_moment = moments[0][...] + moments[1][...]
    later = [part[pl.ds(rows, rows), :] for part in parts]
    for k in range(steps):
        after = reply_moment
        for m in range(steps):
            after = after + jnp.where((pair ^ m) > (pair ^ k), later[m], 0.0)
        returned[k][pl.ds(rows, rows), :] = after


def halves_kernel(steps, place, follows, kept, received, *refs):
    pieces, finals, refs = refs[:steps], refs[steps : 2 * steps], refs[2 * steps :]
    mine, to_other = refs[:2]
    rows = finals[0].shape[0]
    choose(place, finals, {j: (ref, pl.ds(0, rows)) for j, ref in enumerate(refs[2:])})
    member, pair = place[0], place[1]
    half_rows = kept.shape[0] // 2
    piece_rows = half_rows // steps
    first = member == 0
    for k in range(steps):
        start = pl.multiple_of((pair ^ k) * piece_rows, piece_rows)
        for part in range(2):
            rows = pl.ds(part * half_rows + start, piece_rows)
            sums = pieces[k][pl.ds(part * piece_rows, piece_rows), :]
            add_other = first if part else jnp.logical_not(first)
            mine[rows, :] = sums + jnp.where(add_other, received[rows, :], 0.0)
            to_other[rows, :] = sums + jnp.where(add_other, 0.0, kept[rows, :])


def local_terms(first_head, first_row, query, key, value, cotangent, outs, work):
    inner, query_part, key_part, value_part = outs
    weights, mixing, grad_mixing = work
    heads, rows, size = inner.shape
    block = weights.shape[1]
    count = rows // block
    spans = [pl.ds(i * block, block) for i in range(count)]
    for i in range(count):
        weights[i], weights[count + i] = causal_weights(first_row + i * block, block, size)

    def mix(own):
        h, slot = first_head + own, own % 2
        for i in range(count):
            for j in range(i + 1):
                factor = weights[i if i == j else count + i]
                scores = dot(query[h, spans[i]], key[h, spans[j]], LAST_LAST)
                mixing[slot, spans[i], spans[j]] = (scores * factor).astype(BF16)
                scores = dot(cotangent[h, spans[i]], value[h, spans[j]], LAST_LAST)
                grad_mixing[slot, spans[i], spans[j]] = (scores * factor).astype(BF16)

    mix(0)
    for own in range(heads):
        if own + 1 < heads:
            mix(own + 1)
        h, slot = first_head + own, own % 2
        for i in range(count):
            seen = pl.ds(0, (i + 1) * block)
            inner[own, spans[i]] = dot(mixing[slot, spans[i], seen], value[h, seen], LAST_ROWS)
            query_part[own, spans[i]] = dot(
                grad_mixing[slot, spans[i], seen], key[h, seen], LAST_ROWS
            )
            later = pl.ds(i * block, rows - i * block)
            part = dot(grad_mixing[slot, later, spans[i]], query[h, later], ROWS_ROWS)
            key_part[own, spans[i]] = part.astype(key_part.dtype)
            part = dot(mixing[slot, later, spans[i]], cotangent[h, later], ROWS_ROWS)
            value_part[own, spans[i]] = part.astype(value_part.dtype)


def prompt_local_kernel(place, query, key, value, cotangent, reply_key, reply_value, *refs):
    outs, (r_key, r_value, token), work = refs[1:5], refs[5:8], refs[8:11]
    key_buffer, value_buffer, arrived = refs[11:]
    copies = load((reply_key, reply_value), (key_buffer, value_buffer), arrived)
    local_terms(0, place[2], query, key, value, cotangent, outs, work)
    copies[0].wait()
    r_key[...] = by_head(key_buffer[...])
    copies[1].wait()
    r_value[...] = by_head(value_buffer[...])
    token[...] = jnp.zeros_like(token)


def reply_local_kernel(first_head, place, query, key, value, cotangent, follows, *refs):
    outs, token, work = refs[:4], refs[4], refs[5:]
    local_terms(first_head, place[3], query, key, value, cotangent, outs, work)
    token[...] = jnp.zeros_like(token)


def reply_grads_kernel(follows, key_first, value_first, key_second, value_second, *refs):
    grads, token, staged, left = refs[:2], refs[2], refs[3], refs[4]
    token[...] = jnp.zeros_like(token)
    copies = []
    for i, parts in enumerate(((key_first, key_second), (value_first, value_second))):
        staged[i] = by_head(jnp.concatenate([part[...] for part in parts], 0))
        copies.append(pltpu.make_async_copy(staged.at[i], grads[i], left.at[i]))
        copies[-1].start()
    for copy in copies:
        copy.wait()


def causal_weights(first_row, row_total, head_size):
    rows = lax.broadcasted_iota(jnp.int32, (row_total, row_total), 0)
    columns = lax.broadcasted_iota(jnp.int32, (row_total, row_total), 1)
    scale = lax.rsqrt(float(head_size) * ((rows + first_row).astype(F32) + 1.0))
    return jnp.where(rows >= columns, scale, 0.0), scale


def prompt_final_kernel(place, mine, other, *refs):
    parts, (query, key, value, cotangent), grads = refs[:4], refs[4:8], refs[8:12]
    token, before, after, held, staged, left = refs[12:]
    token[...] = jnp.zeros_like(token)
    member, first_row = place[0], place[2]
    heads, rows, size = query.shape
    half = heads // 2
    scale = row_scale(first_row, rows, size)
    copies = []

    def leave(source, target):
        copies.append(pltpu.make_async_copy(source, target, left.at[len(copies)]))
        copies[-1].start()

    for target, offset in ((before, 0), (after, half)):
        for source, base in ((mine, member * half), (other, (1 - member) * half)):
            for j in range(half):
                target[base + j] = source[pl.ds((offset + j) * size, size), :].astype(BF16)
    for i, (array, state, dims) in enumerate(
        (
            (query, before, LAST_ROWS),
            (cotangent, before, LAST_LAST),
            (value, after, LAST_LAST),
            (key, after, LAST_ROWS),
        )
    ):
        for h in range(heads):
            part = dot(array[h], state[h], dims)
            part = scale * part if i < 2 else part
            held[i, h] = (parts[i][h] + part).astype(BF16)
        staged[i] = by_head(held[i])
        leave(staged.at[i], grads[i])
    for copy in copies:
        copy.wait()


def reply_final_kernel(steps, place, follows, *refs):
    pieces, refs = refs[:steps], refs[steps:]
    inner, query_part, (query, cotangent, output, query_grad) = refs[:2], refs[2:4], refs[4:8]
    state, held, staged, left = refs[8:]
    half = inner[0].shape[0]
    pair, first_row, length = place[1], place[3], place[4]
    heads, rows, size = query.shape
    piece_rows = pieces[0].shape[0]
    for k in range(steps):
        start = pl.multiple_of((pair ^ k) * piece_rows, piece_rows)
        state[pl.ds(start, piece_rows), :] = pieces[k][...].astype(BF16)
    scale = row_scale(first_row, rows, size)
    live = lax.broadcasted_iota(jnp.int32, (rows, size), 0) < length
    copies = []

    def finish(i, target):
        staged[i] = by_head(held[i])
        copies.append(pltpu.make_async_copy(staged.at[i], target, left.at[i]))
        copies[-1].start()

    for h in range(heads):
        final = state[pl.ds(h * size, size), :]
        whole = inner[h // half][h % half] + scale * dot(query[h], final, LAST_ROWS)
        held[0, h] = jnp.where(live, whole, 0.0).astype(BF16)
    finish(0, output)
    for h in range(heads):
        final = state[pl.ds(h * size, size), :]
        part = scale * dot(cotangent[h], final, LAST_LAST)
        held[1, h] = (query_part[h // half][h % half] + part).astype(BF16)
    finish(1, query_grad)
    for copy in copies:
        copy.wait()


VMEM = pl.BlockSpec(memory_space=pltpu.VMEM)
HBM = pl.BlockSpec(memory_space=pltpu.HBM)
ANY = pl.BlockSpec(memory_space=pl.ANY)


def call(kernel, scalars, arrays, outs, scratch, name):
    arrays = [
        (spec, pltpu.with_memory_space_constraint(array, pltpu.HBM) if spec is HBM else array)
        for spec, array in arrays
    ]
    return pl.pallas_call(
        kernel,
        out_shape=[out for _, out in outs],
        in_specs=[pl.BlockSpec(memory_space=pltpu.SMEM)] * len(scalars) + [s for s, _ in arrays],
        out_specs=[spec for spec, _ in outs],
        scratch_shapes=scratch,
        compiler_params=pltpu.CompilerParams(vmem_limit_bytes=24 << 20),
        cost_estimate=pl.CostEstimate(flops=1, bytes_accessed=1, transcendentals=0),
        name=name,
    )(*scalars, *[array for _, array in arrays])


def held_in(spec, arrays):
    return [(spec, array) for array in arrays]


def shards(
    prompt_query,
    prompt_key,
    prompt_value,
    prompt_cotangent,
    reply_query,
    reply_key,
    reply_value,
    reply_cotangent,
    reply_weight,
    reply_length,
):
    rows, heads, size = prompt_query.shape
    reply_query, reply_key = reply_query[0], reply_key[0]
    reply_value, reply_cotangent = reply_value[0], reply_cotangent[0]
    reply_rows, reply_heads = reply_query.shape[:2]
    block_count = lax.axis_size(PLANE)
    steps = lax.axis_size("resp")
    assert block_count == 2 * steps and steps & (steps - 1) == 0
    block_index = lax.axis_index(PLANE)
    resp_index = lax.axis_index("resp")
    pair_index, member = block_index // 2, block_index % 2
    half_rows = heads // 2 * size
    piece_rows = half_rows // steps
    place = jnp.stack(
        [
            member,
            pair_index,
            block_index * rows,
            block_count * rows,
            reply_length[0],
            resp_index,
        ]
    ).astype(jnp.int32)
    shape = jax.ShapeDtypeStruct
    prompt_bf16 = shape((rows, heads, size), BF16)
    reply_bf16 = shape((reply_rows, reply_heads, size), BF16)
    prompt_held = shape((heads, rows, size), BF16)
    reply_held = shape((reply_heads, reply_rows, size), BF16)
    piece = shape((piece_rows, size), F32)
    two_pieces = shape((2 * piece_rows, size), F32)
    two_halves = shape((2 * half_rows, size), F32)

    def scratch(held, count=None):
        return pltpu.VMEM(held.shape if count is None else (count, *held.shape), held.dtype)

    sent, kept, key, value, query, cotangent, r_query, r_cotangent, *moments = call(
        functools.partial(moments_kernel, steps),
        [place, reply_weight],
        held_in(
            HBM,
            [prompt_key, prompt_value, prompt_query, prompt_cotangent, reply_query, reply_cotangent],
        ),
        held_in(
            VMEM, [two_halves] * 2 + [prompt_held] * 4 + [reply_held] * 2 + [piece] * steps
        ),
        [scratch(prompt_bf16)] * 4
        + [scratch(reply_bf16)] * 2
        + [scratch(prompt_held), scratch(reply_held)]
        + [pltpu.VMEM((reply_heads * size, size), F32), pltpu.VMEM((reply_rows, size), F32)]
        + [pltpu.SemaphoreType.DMA((6,))],
        "moments",
    )
    received = pair_step(sent)
    moments = plane_exchange(moments)
    pieces = call(
        functools.partial(pair_kernel, steps),
        [place],
        held_in(VMEM, [kept, received]),
        held_in(VMEM, [two_pieces] * steps),
        [],
        "pair_sums",
    )
    parts = plane_exchange(pieces)
    half_heads = reply_heads // 2
    half_reply = shape((half_heads, reply_rows, size), F32)
    half_held = shape((half_heads, reply_rows, size), BF16)
    prompt_wide = shape((heads, rows, size), F32)
    token = shape((8, 128), F32)

    def work(total):
        block = min(BLOCK, total)
        mixing = pltpu.VMEM((2, total, total), BF16)
        return [pltpu.VMEM((2 * (total // block), block, block), F32), mixing, mixing]

    prompt_arrays = held_in(VMEM, [query, key, value, cotangent])
    *prompt_parts, r_key, r_value, done = call(
        prompt_local_kernel,
        [place],
        prompt_arrays + held_in(HBM, [reply_key, reply_value]) + held_in(ANY, pieces[:1]),
        held_in(VMEM, [prompt_wide] * 4 + [reply_held] * 2 + [token]),
        work(rows) + [scratch(reply_bf16)] * 2 + [pltpu.SemaphoreType.DMA((2,))],
        "prompt_local",
    )
    stays, leaves, done = call(
        functools.partial(choose_kernel, steps),
        [place],
        held_in(ANY, [done]) + held_in(VMEM, moments),
        held_in(VMEM, [shape((steps // 2 * piece_rows, size), F32)] * 2 + [token]),
        [],
        "choose_moments",
    )
    reply_arrays = held_in(VMEM, [r_query, r_key, r_value, r_cotangent])
    reply_terms = held_in(VMEM, [half_reply] * 2 + [half_held] * 2 + [token])
    inner_first, part_first, key_first, value_first, done = call(
        functools.partial(reply_local_kernel, 0),
        [place],
        reply_arrays + held_in(ANY, [done]),
        reply_terms,
        work(reply_rows),
        "reply_local_first",
    )
    masks = resp_masks(steps)
    for mask in masks[:-1]:
        rows_left = stays.shape[0] // 2
        stays, leaves = call(
            halve_kernel,
            [],
            held_in(ANY, [done]) + held_in(VMEM, [stays, resp_step(leaves, mask)]),
            held_in(VMEM, [shape((rows_left, size), F32)] * 2),
            [],
            "reply_moments",
        )
    inner_second, part_second, key_second, value_second, done = call(
        functools.partial(reply_local_kernel, half_heads),
        [place],
        reply_arrays + held_in(ANY, [leaves]),
        reply_terms,
        work(reply_rows),
        "reply_local_second",
    )
    final, *returned = call(
        functools.partial(prefix_kernel, steps),
        [place],
        held_in(ANY, [done]) + held_in(VMEM, [*parts, stays, resp_step(leaves, masks[-1])]),
        held_in(VMEM, [piece] + [two_pieces] * steps),
        [],
        "prefix_sums",
    )
    finals = resp_gather(final)
    returned = plane_exchange(returned)
    reply_dkey, reply_dvalue, done = call(
        reply_grads_kernel,
        [],
        held_in(ANY, [final])
        + held_in(VMEM, [key_first, value_first, key_second, value_second]),
        held_in(HBM, [reply_bf16] * 2) + held_in(VMEM, [token]),
        [scratch(reply_bf16, 2), pltpu.SemaphoreType.DMA((2,))],
        "reply_grads",
    )
    mine, to_other, *finals = call(
        functools.partial(halves_kernel, steps),
        [place],
        held_in(ANY, [done]) + held_in(VMEM, [kept, received, *returned, *finals]),
        held_in(VMEM, [two_halves] * 2 + [piece] * steps),
        [],
        "halves",
    )
    finals = plane_exchange(finals)
    other = pair_step(to_other)
    *prompt_results, done = call(
        prompt_final_kernel,
        [place],
        held_in(VMEM, [mine, other, *prompt_parts]) + prompt_arrays,
        held_in(HBM, [prompt_bf16] * 4) + held_in(VMEM, [token]),
        [pltpu.VMEM((heads, size, size), BF16)] * 2
        + [scratch(prompt_held, 4), scratch(prompt_bf16, 4)]
        + [pltpu.SemaphoreType.DMA((4,))],
        "prompt_final",
    )
    prompt_output, prompt_dquery, prompt_dkey, prompt_dvalue = prompt_results
    reply_output, reply_dquery = call(
        functools.partial(reply_final_kernel, steps),
        [place],
        held_in(ANY, [done])
        + held_in(VMEM, [*finals, inner_first, inner_second, part_first, part_second])
        + held_in(VMEM, [r_query, r_cotangent]),
        held_in(HBM, [reply_bf16] * 2),
        [
            pltpu.VMEM((reply_heads * size, size), BF16),
            scratch(reply_held, 2),
            scratch(reply_bf16, 2),
            pltpu.SemaphoreType.DMA((2,)),
        ],
        "reply_final",
    )
    return (
        prompt_output,
        reply_output[None],
        prompt_dquery,
        prompt_dkey,
        prompt_dvalue,
        reply_dquery[None],
        reply_dkey[None],
        reply_dvalue[None],
    )


def solution(mesh):
    prompt = P(PLANE, "resp", None)
    reply = P("resp", None, PLANE, None)
    return jax.shard_map(
        shards,
        mesh=mesh,
        in_specs=(prompt,) * 4 + (reply,) * 4 + (P("resp"),) * 2,
        out_specs=(prompt, reply, prompt, prompt, prompt, reply, reply, reply),
        check_vma=False,
    )
```

```python
import functools

import jax
import jax.numpy as jnp
from jax import lax
from jax.experimental import pallas as pl
from jax.experimental.pallas import tpu as pltpu
from jax.sharding import PartitionSpec as P

PLANE = ("ctx", "head")
BLOCK = 256
CHUNK = 64
F32 = jnp.float32
BF16 = jnp.bfloat16
ROWS_ROWS = (((0,), (0,)), ((), ()))
LAST_LAST = (((1,), (1,)), ((), ()))
LAST_ROWS = (((1,), (0,)), ((), ()))


def pair_step(block):
    count = lax.axis_size(PLANE)
    return lax.ppermute(block, PLANE, [(b, b ^ 1) for b in range(count)])


def plane_exchange(pieces):
    count = lax.axis_size(PLANE)
    moved = [pieces[0]]
    for k in range(1, len(pieces)):
        moved.append(lax.ppermute(pieces[k], PLANE, [(b, b ^ (2 * k)) for b in range(count)]))
    return moved


def resp_masks(count):
    return [3 if mask == 2 else mask for mask in (1 << i for i in range(count.bit_length() - 1))]


def resp_step(array, mask):
    count = lax.axis_size("resp")
    return lax.ppermute(array, "resp", [(z, z ^ mask) for z in range(count)])


def resp_gather(piece):
    held = {0: piece}
    for mask in resp_masks(lax.axis_size("resp")):
        held.update({j ^ mask: resp_step(array, mask) for j, array in list(held.items())})
    return [held[j] for j in range(len(held))]


def halving_order(count):
    order = [0]
    for mask in reversed(resp_masks(count)):
        order = order + [j ^ mask for j in order]
    return order


def dot(a, b, dims):
    return lax.dot_general(a, b, dims, preferred_element_type=F32)


def row_scale(first_row, row_total, head_size):
    rows = lax.broadcasted_iota(jnp.int32, (row_total, head_size), 0) + first_row
    return lax.rsqrt(float(head_size) * (rows.astype(F32) + 1.0))


def to_heads(target, source, factor=None, scaled=None):
    rows = source.shape[0]
    chunk = CHUNK if rows % CHUNK == 0 else rows

    def one(i, carry):
        start = pl.multiple_of(i * chunk, chunk)
        span = pl.ds(start, chunk)
        part = jnp.swapaxes(source[span], 0, 1)
        if factor is not None:
            product = (part.astype(F32) * factor(start, chunk)[None]).astype(BF16)
            if scaled is None:
                part = product
            else:
                scaled[:, span, :] = product
        target[:, span, :] = part
        return carry

    lax.fori_loop(0, rows // chunk, one, 0)


def by_head(array):
    return jnp.swapaxes(array, 0, 1)


def load(sources, buffers, arrived):
    copies = []
    for i, (source, buffer) in enumerate(zip(sources, buffers)):
        copies.append(pltpu.make_async_copy(source, buffer, arrived.at[i]))
        copies[-1].start()
    return copies


def moments_kernel(steps, place, weight, *refs):
    sources, refs = refs[:6], refs[6:]
    sent, kept, key, value, query, cotangent, r_query, r_cotangent = refs[:8]
    pieces, refs = refs[8 : 8 + steps], refs[8 + steps :]
    buffers, (scaled, r_scaled, r_moment, arrived) = refs[:6], refs[6:]
    copies = load(sources, buffers, arrived)
    member, first_row, reply_first, length = (place[i] for i in (0, 2, 3, 4))
    heads, rows, size = query.shape
    half = heads // 2
    halves = ((sent, (1 - member) * half), (kept, member * half))
    for i, target in enumerate((key, value)):
        copies[i].wait()
        to_heads(target, buffers[i])
    for target, base in halves:

        def state(j, carry, target=target, base=base):
            h = base + j
            target[pl.ds(j * size, size), :] = dot(key[h], value[h], ROWS_ROWS)
            return carry

        lax.fori_loop(0, half, state, 0, unroll=True)
    copies[2].wait()
    to_heads(
        query, buffers[2], lambda start, total: row_scale(first_row + start, total, size), scaled
    )
    copies[3].wait()
    to_heads(cotangent, buffers[3])
    for target, base in halves:

        def moment(j, carry, target=target, base=base):
            h = base + j
            target[pl.ds((half + j) * size, size), :] = dot(scaled[h], cotangent[h], ROWS_ROWS)
            return carry

        lax.fori_loop(0, half, moment, 0, unroll=True)
    def live_weight(start, total):
        rows_at = lax.broadcasted_iota(jnp.int32, (total, size), 0) + start
        return jnp.where(rows_at < length, weight[0], 0.0)

    copies[4].wait()
    to_heads(
        r_query,
        buffers[4],
        lambda start, total: row_scale(reply_first + start, total, size),
        r_scaled,
    )
    copies[5].wait()
    to_heads(r_cotangent, buffers[5], live_weight)
    for h in range(r_query.shape[0]):
        r_moment[pl.ds(h * size, size), :] = dot(r_scaled[h], r_cotangent[h], ROWS_ROWS)
    piece_rows = pieces[0].shape[0]
    for k in range(steps):
        start = pl.multiple_of((place[1] ^ k) * piece_rows, piece_rows)
        pieces[k][...] = r_moment[pl.ds(start, piece_rows), :]


def pair_kernel(steps, place, kept, received, *pieces):
    pair = place[1]
    half_rows = kept.shape[0] // 2
    piece_rows = half_rows // steps
    for k in range(steps):
        start = pl.multiple_of((pair ^ k) * piece_rows, piece_rows)
        for part in range(2):
            source = pl.ds(part * half_rows + start, piece_rows)
            pieces[k][pl.ds(part * piece_rows, piece_rows), :] = kept[source, :] + received[source, :]


def choose(place, pieces, targets):
    start = place[1] ^ place[5]
    for j, (target, rows) in targets.items():
        chosen = pieces[0][...]
        for k in range(1, len(pieces)):
            chosen = jnp.where((start ^ j) == k, pieces[k][...], chosen)
        target[rows, :] = chosen


def choose_kernel(steps, place, follows, *refs):
    pieces, (stays, leaves, token) = refs[:steps], refs[steps:]
    token[...] = jnp.zeros_like(token)
    rows = pieces[0].shape[0]
    order, half = halving_order(steps), steps // 2
    targets = {
        j: (leaves if i >= half else stays, pl.ds(i % half * rows, rows)) for i, j in enumerate(order)
    }
    choose(place, pieces, targets)


def halve_kernel(follows, mine, other, stays, leaves):
    rows = stays.shape[0]
    stays[...] = mine[pl.ds(0, rows), :] + other[pl.ds(0, rows), :]
    leaves[...] = mine[pl.ds(rows, rows), :] + other[pl.ds(rows, rows), :]


def prefix_kernel(steps, place, follows, *refs):
    parts, moments, refs = refs[:steps], refs[steps : steps + 2], refs[steps + 2 :]
    final, returned = refs[0], refs[1:]
    pair = place[1]
    rows = final.shape[0]
    states = [part[pl.ds(0, rows), :] for part in parts]
    total = states[0]
    for k in range(1, steps):
        total = total + states[k]
    final[...] = total
    for k in range(steps):
        before = jnp.zeros_like(total)
        for m in range(steps):
            before = before + jnp.where((pair ^ m) < (pair ^ k), states[m], 0.0)
        returned[k][pl.ds(0, rows), :] = before
    reply_moment = moments[0][...] + moments[1][...]
    later = [part[pl.ds(rows, rows), :] for part in parts]
    for k in range(steps):
        after = reply_moment
        for m in range(steps):
            after = after + jnp.where((pair ^ m) > (pair ^ k), later[m], 0.0)
        returned[k][pl.ds(rows, rows), :] = after


def halves_kernel(steps, place, follows, kept, received, *refs):
    pieces, finals, refs = refs[:steps], refs[steps : 2 * steps], refs[2 * steps :]
    mine, to_other = refs[:2]
    rows = finals[0].shape[0]
    choose(place, finals, {j: (ref, pl.ds(0, rows)) for j, ref in enumerate(refs[2:])})
    member, pair = place[0], place[1]
    half_rows = kept.shape[0] // 2
    piece_rows = half_rows // steps
    first = member == 0
    for k in range(steps):
        start = pl.multiple_of((pair ^ k) * piece_rows, piece_rows)
        for part in range(2):
            rows = pl.ds(part * half_rows + start, piece_rows)
            sums = pieces[k][pl.ds(part * piece_rows, piece_rows), :]
            add_other = first if part else jnp.logical_not(first)
            mine[rows, :] = sums + jnp.where(add_other, received[rows, :], 0.0)
            to_other[rows, :] = sums + jnp.where(add_other, 0.0, kept[rows, :])


def local_terms(first_head, first_row, query, key, value, cotangent, outs, work):
    inner, query_part, key_part, value_part = outs
    weights, mixing, grad_mixing = work
    heads, rows, size = inner.shape
    block = weights.shape[1]
    count = rows // block
    spans = [pl.ds(i * block, block) for i in range(count)]
    for i in range(count):
        weights[i], weights[count + i] = causal_weights(first_row + i * block, block, size)

    def mix(own):
        h, slot = first_head + own, own % 2
        for i in range(count):
            for j in range(i + 1):
                factor = weights[i if i == j else count + i]
                scores = dot(query[h, spans[i]], key[h, spans[j]], LAST_LAST)
                mixing[slot, spans[i], spans[j]] = (scores * factor).astype(BF16)
                scores = dot(cotangent[h, spans[i]], value[h, spans[j]], LAST_LAST)
                grad_mixing[slot, spans[i], spans[j]] = (scores * factor).astype(BF16)

    mix(0)
    for own in range(heads):
        if own + 1 < heads:
            mix(own + 1)
        h, slot = first_head + own, own % 2
        for i in range(count):
            seen = pl.ds(0, (i + 1) * block)
            inner[own, spans[i]] = dot(mixing[slot, spans[i], seen], value[h, seen], LAST_ROWS)
            query_part[own, spans[i]] = dot(
                grad_mixing[slot, spans[i], seen], key[h, seen], LAST_ROWS
            )
            later = pl.ds(i * block, rows - i * block)
            part = dot(grad_mixing[slot, later, spans[i]], query[h, later], ROWS_ROWS)
            key_part[own, spans[i]] = part.astype(key_part.dtype)
            part = dot(mixing[slot, later, spans[i]], cotangent[h, later], ROWS_ROWS)
            value_part[own, spans[i]] = part.astype(value_part.dtype)


def prompt_local_kernel(place, query, key, value, cotangent, reply_key, reply_value, *refs):
    outs, (r_key, r_value, token), work = refs[1:5], refs[5:8], refs[8:11]
    key_buffer, value_buffer, arrived = refs[11:]
    copies = load((reply_key, reply_value), (key_buffer, value_buffer), arrived)
    local_terms(0, place[2], query, key, value, cotangent, outs, work)
    copies[0].wait()
    r_key[...] = by_head(key_buffer[...])
    copies[1].wait()
    r_value[...] = by_head(value_buffer[...])
    token[...] = jnp.zeros_like(token)


def reply_local_kernel(first_head, place, query, key, value, cotangent, follows, *refs):
    outs, token, work = refs[:4], refs[4], refs[5:]
    local_terms(first_head, place[3], query, key, value, cotangent, outs, work)
    token[...] = jnp.zeros_like(token)


def reply_grads_kernel(follows, key_first, value_first, key_second, value_second, *refs):
    grads, token, staged, left = refs[:2], refs[2], refs[3], refs[4]
    token[...] = jnp.zeros_like(token)
    copies = []
    for i, parts in enumerate(((key_first, key_second), (value_first, value_second))):
        staged[i] = by_head(jnp.concatenate([part[...] for part in parts], 0))
        copies.append(pltpu.make_async_copy(staged.at[i], grads[i], left.at[i]))
        copies[-1].start()
    for copy in copies:
        copy.wait()


def causal_weights(first_row, row_total, head_size):
    rows = lax.broadcasted_iota(jnp.int32, (row_total, row_total), 0)
    columns = lax.broadcasted_iota(jnp.int32, (row_total, row_total), 1)
    scale = lax.rsqrt(float(head_size) * ((rows + first_row).astype(F32) + 1.0))
    return jnp.where(rows >= columns, scale, 0.0), scale


def prompt_final_kernel(place, mine, other, *refs):
    parts, (query, key, value, cotangent), grads = refs[:4], refs[4:8], refs[8:12]
    token, before, after, held, staged, left = refs[12:]
    token[...] = jnp.zeros_like(token)
    member, first_row = place[0], place[2]
    heads, rows, size = query.shape
    half = heads // 2
    scale = row_scale(first_row, rows, size)
    copies = []

    def leave(source, target):
        copies.append(pltpu.make_async_copy(source, target, left.at[len(copies)]))
        copies[-1].start()

    for target, offset in ((before, 0), (after, half)):
        for source, base in ((mine, member * half), (other, (1 - member) * half)):
            for j in range(half):
                target[base + j] = source[pl.ds((offset + j) * size, size), :].astype(BF16)
    for i, (array, state, dims) in enumerate(
        (
            (query, before, LAST_ROWS),
            (cotangent, before, LAST_LAST),
            (value, after, LAST_LAST),
            (key, after, LAST_ROWS),
        )
    ):
        for h in range(heads):
            part = dot(array[h], state[h], dims)
            part = scale * part if i < 2 else part
            held[i, h] = (parts[i][h] + part).astype(BF16)
        staged[i] = by_head(held[i])
        leave(staged.at[i], grads[i])
    for copy in copies:
        copy.wait()


def reply_final_kernel(steps, place, follows, *refs):
    pieces, refs = refs[:steps], refs[steps:]
    inner, query_part, (query, cotangent, output, query_grad) = refs[:2], refs[2:4], refs[4:8]
    state, held, staged, left = refs[8:]
    half = inner[0].shape[0]
    pair, first_row, length = place[1], place[3], place[4]
    heads, rows, size = query.shape
    piece_rows = pieces[0].shape[0]
    for k in range(steps):
        start = pl.multiple_of((pair ^ k) * piece_rows, piece_rows)
        state[pl.ds(start, piece_rows), :] = pieces[k][...].astype(BF16)
    scale = row_scale(first_row, rows, size)
    live = lax.broadcasted_iota(jnp.int32, (rows, size), 0) < length
    copies = []

    def finish(i, target):
        part = rows // 4
        for start in range(0, rows, part):
            span = pl.ds(start, part)
            staged[i, span] = by_head(held[i, :, span])
            copies.append(
                pltpu.make_async_copy(staged.at[i, span], target.at[span], left.at[len(copies)])
            )
            copies[-1].start()

    for h in range(heads):
        final = state[pl.ds(h * size, size), :]
        whole = inner[h // half][h % half] + scale * dot(query[h], final, LAST_ROWS)
        held[0, h] = jnp.where(live, whole, 0.0).astype(BF16)
    finish(0, output)
    for h in range(heads):
        final = state[pl.ds(h * size, size), :]
        part = scale * dot(cotangent[h], final, LAST_LAST)
        held[1, h] = (query_part[h // half][h % half] + part).astype(BF16)
    finish(1, query_grad)
    for copy in copies:
        copy.wait()


VMEM = pl.BlockSpec(memory_space=pltpu.VMEM)
HBM = pl.BlockSpec(memory_space=pltpu.HBM)
ANY = pl.BlockSpec(memory_space=pl.ANY)


def call(kernel, scalars, arrays, outs, scratch, name):
    arrays = [
        (spec, pltpu.with_memory_space_constraint(array, pltpu.HBM) if spec is HBM else array)
        for spec, array in arrays
    ]
    return pl.pallas_call(
        kernel,
        out_shape=[out for _, out in outs],
        in_specs=[pl.BlockSpec(memory_space=pltpu.SMEM)] * len(scalars) + [s for s, _ in arrays],
        out_specs=[spec for spec, _ in outs],
        scratch_shapes=scratch,
        compiler_params=pltpu.CompilerParams(vmem_limit_bytes=24 << 20),
        cost_estimate=pl.CostEstimate(flops=1, bytes_accessed=1, transcendentals=0),
        name=name,
    )(*scalars, *[array for _, array in arrays])


def held_in(spec, arrays):
    return [(spec, array) for array in arrays]


def shards(
    prompt_query,
    prompt_key,
    prompt_value,
    prompt_cotangent,
    reply_query,
    reply_key,
    reply_value,
    reply_cotangent,
    reply_weight,
    reply_length,
):
    rows, heads, size = prompt_query.shape
    reply_query, reply_key = reply_query[0], reply_key[0]
    reply_value, reply_cotangent = reply_value[0], reply_cotangent[0]
    reply_rows, reply_heads = reply_query.shape[:2]
    block_count = lax.axis_size(PLANE)
    steps = lax.axis_size("resp")
    assert block_count == 2 * steps and steps & (steps - 1) == 0
    block_index = lax.axis_index(PLANE)
    resp_index = lax.axis_index("resp")
    pair_index, member = block_index // 2, block_index % 2
    half_rows = heads // 2 * size
    piece_rows = half_rows // steps
    place = jnp.stack(
        [
            member,
            pair_index,
            block_index * rows,
            block_count * rows,
            reply_length[0],
            resp_index,
        ]
    ).astype(jnp.int32)
    shape = jax.ShapeDtypeStruct
    prompt_bf16 = shape((rows, heads, size), BF16)
    reply_bf16 = shape((reply_rows, reply_heads, size), BF16)
    prompt_held = shape((heads, rows, size), BF16)
    reply_held = shape((reply_heads, reply_rows, size), BF16)
    piece = shape((piece_rows, size), F32)
    two_pieces = shape((2 * piece_rows, size), F32)
    two_halves = shape((2 * half_rows, size), F32)

    def scratch(held, count=None):
        return pltpu.VMEM(held.shape if count is None else (count, *held.shape), held.dtype)

    sent, kept, key, value, query, cotangent, r_query, r_cotangent, *moments = call(
        functools.partial(moments_kernel, steps),
        [place, reply_weight],
        held_in(
            HBM,
            [prompt_key, prompt_value, prompt_query, prompt_cotangent, reply_query, reply_cotangent],
        ),
        held_in(
            VMEM, [two_halves] * 2 + [prompt_held] * 4 + [reply_held] * 2 + [piece] * steps
        ),
        [scratch(prompt_bf16)] * 4
        + [scratch(reply_bf16)] * 2
        + [scratch(prompt_held), scratch(reply_held)]
        + [pltpu.VMEM((reply_heads * size, size), F32)]
        + [pltpu.SemaphoreType.DMA((6,))],
        "moments",
    )
    received = pair_step(sent)
    moments = plane_exchange(moments)
    pieces = call(
        functools.partial(pair_kernel, steps),
        [place],
        held_in(VMEM, [kept, received]),
        held_in(VMEM, [two_pieces] * steps),
        [],
        "pair_sums",
    )
    parts = plane_exchange(pieces)
    half_heads = reply_heads // 2
    half_reply = shape((half_heads, reply_rows, size), F32)
    half_held = shape((half_heads, reply_rows, size), BF16)
    prompt_wide = shape((heads, rows, size), F32)
    token = shape((8, 128), F32)

    def work(total):
        block = min(BLOCK, total)
        mixing = pltpu.VMEM((2, total, total), BF16)
        return [pltpu.VMEM((2 * (total // block), block, block), F32), mixing, mixing]

    prompt_arrays = held_in(VMEM, [query, key, value, cotangent])
    *prompt_parts, r_key, r_value, done = call(
        prompt_local_kernel,
        [place],
        prompt_arrays + held_in(HBM, [reply_key, reply_value]) + held_in(ANY, pieces[:1]),
        held_in(VMEM, [prompt_wide] * 4 + [reply_held] * 2 + [token]),
        work(rows) + [scratch(reply_bf16)] * 2 + [pltpu.SemaphoreType.DMA((2,))],
        "prompt_local",
    )
    stays, leaves, done = call(
        functools.partial(choose_kernel, steps),
        [place],
        held_in(ANY, [done]) + held_in(VMEM, moments),
        held_in(VMEM, [shape((steps // 2 * piece_rows, size), F32)] * 2 + [token]),
        [],
        "choose_moments",
    )
    reply_arrays = held_in(VMEM, [r_query, r_key, r_value, r_cotangent])
    reply_terms = held_in(VMEM, [half_reply] * 2 + [half_held] * 2 + [token])
    inner_first, part_first, key_first, value_first, done = call(
        functools.partial(reply_local_kernel, 0),
        [place],
        reply_arrays + held_in(ANY, [done]),
        reply_terms,
        work(reply_rows),
        "reply_local_first",
    )
    masks = resp_masks(steps)
    for mask in masks[:-1]:
        rows_left = stays.shape[0] // 2
        stays, leaves = call(
            halve_kernel,
            [],
            held_in(ANY, [done]) + held_in(VMEM, [stays, resp_step(leaves, mask)]),
            held_in(VMEM, [shape((rows_left, size), F32)] * 2),
            [],
            "reply_moments",
        )
    inner_second, part_second, key_second, value_second, done = call(
        functools.partial(reply_local_kernel, half_heads),
        [place],
        reply_arrays + held_in(ANY, [leaves]),
        reply_terms,
        work(reply_rows),
        "reply_local_second",
    )
    final, *returned = call(
        functools.partial(prefix_kernel, steps),
        [place],
        held_in(ANY, [done]) + held_in(VMEM, [*parts, stays, resp_step(leaves, masks[-1])]),
        held_in(VMEM, [piece] + [two_pieces] * steps),
        [],
        "prefix_sums",
    )
    finals = resp_gather(final)
    returned = plane_exchange(returned)
    reply_dkey, reply_dvalue, done = call(
        reply_grads_kernel,
        [],
        held_in(ANY, [final])
        + held_in(VMEM, [key_first, value_first, key_second, value_second]),
        held_in(HBM, [reply_bf16] * 2) + held_in(VMEM, [token]),
        [scratch(reply_bf16, 2), pltpu.SemaphoreType.DMA((2,))],
        "reply_grads",
    )
    mine, to_other, *finals = call(
        functools.partial(halves_kernel, steps),
        [place],
        held_in(ANY, [done]) + held_in(VMEM, [kept, received, *returned, *finals]),
        held_in(VMEM, [two_halves] * 2 + [piece] * steps),
        [],
        "halves",
    )
    finals = plane_exchange(finals)
    other = pair_step(to_other)
    *prompt_results, done = call(
        prompt_final_kernel,
        [place],
        held_in(VMEM, [mine, other, *prompt_parts]) + prompt_arrays,
        held_in(HBM, [prompt_bf16] * 4) + held_in(VMEM, [token]),
        [pltpu.VMEM((heads, size, size), BF16)] * 2
        + [scratch(prompt_held, 4), scratch(prompt_bf16, 4)]
        + [pltpu.SemaphoreType.DMA((4,))],
        "prompt_final",
    )
    prompt_output, prompt_dquery, prompt_dkey, prompt_dvalue = prompt_results
    reply_output, reply_dquery = call(
        functools.partial(reply_final_kernel, steps),
        [place],
        held_in(ANY, [done])
        + held_in(VMEM, [*finals, inner_first, inner_second, part_first, part_second])
        + held_in(VMEM, [r_query, r_cotangent]),
        held_in(HBM, [reply_bf16] * 2),
        [
            pltpu.VMEM((reply_heads * size, size), BF16),
            scratch(reply_held, 2),
            scratch(reply_bf16, 2),
            pltpu.SemaphoreType.DMA((8,)),
        ],
        "reply_final",
    )
    return (
        prompt_output,
        reply_output[None],
        prompt_dquery,
        prompt_dkey,
        prompt_dvalue,
        reply_dquery[None],
        reply_dkey[None],
        reply_dvalue[None],
    )


def solution(mesh):
    prompt = P(PLANE, "resp", None)
    reply = P("resp", None, PLANE, None)
    return jax.shard_map(
        shards,
        mesh=mesh,
        in_specs=(prompt,) * 4 + (reply,) * 4 + (P("resp"),) * 2,
        out_specs=(prompt, reply, prompt, prompt, prompt, reply, reply, reply),
        check_vma=False,
    )
```

```python
import functools

import jax
import jax.numpy as jnp
from jax import lax
from jax.experimental import pallas as pl
from jax.experimental.pallas import tpu as pltpu
from jax.sharding import PartitionSpec as P

PLANE = ("ctx", "head")
BLOCK = 256
CHUNK = 64
F32 = jnp.float32
BF16 = jnp.bfloat16
ROWS_ROWS = (((0,), (0,)), ((), ()))
LAST_LAST = (((1,), (1,)), ((), ()))
LAST_ROWS = (((1,), (0,)), ((), ()))


def pair_step(block):
    count = lax.axis_size(PLANE)
    return lax.ppermute(block, PLANE, [(b, b ^ 1) for b in range(count)])


def plane_exchange(pieces):
    count = lax.axis_size(PLANE)
    moved = [pieces[0]]
    for k in range(1, len(pieces)):
        moved.append(lax.ppermute(pieces[k], PLANE, [(b, b ^ (2 * k)) for b in range(count)]))
    return moved


def resp_masks(count):
    return [3 if mask == 2 else mask for mask in (1 << i for i in range(count.bit_length() - 1))]


def resp_step(array, mask):
    count = lax.axis_size("resp")
    return lax.ppermute(array, "resp", [(z, z ^ mask) for z in range(count)])


def resp_gather(piece):
    held = {0: piece}
    for mask in resp_masks(lax.axis_size("resp")):
        held.update({j ^ mask: resp_step(array, mask) for j, array in list(held.items())})
    return [held[j] for j in range(len(held))]


def halving_order(count):
    order = [0]
    for mask in reversed(resp_masks(count)):
        order = order + [j ^ mask for j in order]
    return order


def dot(a, b, dims):
    return lax.dot_general(a, b, dims, preferred_element_type=F32)


def row_scale(first_row, row_total, head_size):
    rows = lax.broadcasted_iota(jnp.int32, (row_total, head_size), 0) + first_row
    return lax.rsqrt(float(head_size) * (rows.astype(F32) + 1.0))


def to_heads(target, source, factor=None, scaled=None):
    rows = source.shape[0]
    chunk = CHUNK if rows % CHUNK == 0 else rows

    def one(i, carry):
        start = pl.multiple_of(i * chunk, chunk)
        span = pl.ds(start, chunk)
        part = jnp.swapaxes(source[span], 0, 1)
        if factor is not None:
            product = (part.astype(F32) * factor(start, chunk)[None]).astype(BF16)
            if scaled is None:
                part = product
            else:
                scaled[:, span, :] = product
        target[:, span, :] = part
        return carry

    lax.fori_loop(0, rows // chunk, one, 0)


def by_head(array):
    return jnp.swapaxes(array, 0, 1)


def load(sources, buffers, arrived):
    copies = []
    for i, (source, buffer) in enumerate(zip(sources, buffers)):
        copies.append(pltpu.make_async_copy(source, buffer, arrived.at[i]))
        copies[-1].start()
    return copies


def moments_kernel(steps, place, weight, *refs):
    sources, refs = refs[:6], refs[6:]
    sent, kept, key, value, query, cotangent, r_query, r_cotangent = refs[:8]
    pieces, refs = refs[8 : 8 + steps], refs[8 + steps :]
    buffers, (scaled, r_scaled, r_moment, arrived) = refs[:6], refs[6:]
    copies = load(sources, buffers, arrived)
    member, first_row, reply_first, length = (place[i] for i in (0, 2, 3, 4))
    heads, rows, size = query.shape
    half = heads // 2
    halves = ((sent, (1 - member) * half), (kept, member * half))
    for i, target in enumerate((key, value)):
        copies[i].wait()
        to_heads(target, buffers[i])
    for target, base in halves:

        def state(j, carry, target=target, base=base):
            h = base + j
            target[pl.ds(j * size, size), :] = dot(key[h], value[h], ROWS_ROWS)
            return carry

        lax.fori_loop(0, half, state, 0, unroll=True)
    copies[2].wait()
    to_heads(
        query, buffers[2], lambda start, total: row_scale(first_row + start, total, size), scaled
    )
    copies[3].wait()
    to_heads(cotangent, buffers[3])
    for target, base in halves:

        def moment(j, carry, target=target, base=base):
            h = base + j
            target[pl.ds((half + j) * size, size), :] = dot(scaled[h], cotangent[h], ROWS_ROWS)
            return carry

        lax.fori_loop(0, half, moment, 0, unroll=True)
    def live_weight(start, total):
        rows_at = lax.broadcasted_iota(jnp.int32, (total, size), 0) + start
        return jnp.where(rows_at < length, weight[0], 0.0)

    copies[4].wait()
    to_heads(
        r_query,
        buffers[4],
        lambda start, total: row_scale(reply_first + start, total, size),
        r_scaled,
    )
    copies[5].wait()
    to_heads(r_cotangent, buffers[5], live_weight)
    for h in range(r_query.shape[0]):
        r_moment[pl.ds(h * size, size), :] = dot(r_scaled[h], r_cotangent[h], ROWS_ROWS)
    piece_rows = pieces[0].shape[0]
    for k in range(steps):
        start = pl.multiple_of((place[1] ^ k) * piece_rows, piece_rows)
        pieces[k][...] = r_moment[pl.ds(start, piece_rows), :]


def pair_kernel(steps, place, kept, received, *pieces):
    pair = place[1]
    half_rows = kept.shape[0] // 2
    piece_rows = half_rows // steps
    for k in range(steps):
        start = pl.multiple_of((pair ^ k) * piece_rows, piece_rows)
        for part in range(2):
            source = pl.ds(part * half_rows + start, piece_rows)
            pieces[k][pl.ds(part * piece_rows, piece_rows), :] = kept[source, :] + received[source, :]


def choose(place, pieces, targets):
    start = place[1] ^ place[5]
    for j, (target, rows) in targets.items():
        chosen = pieces[0][...]
        for k in range(1, len(pieces)):
            chosen = jnp.where((start ^ j) == k, pieces[k][...], chosen)
        target[rows, :] = chosen


def choose_kernel(steps, place, follows, *refs):
    pieces, (stays, leaves, token) = refs[:steps], refs[steps:]
    token[...] = jnp.zeros_like(token)
    rows = pieces[0].shape[0]
    order, half = halving_order(steps), steps // 2
    targets = {
        j: (leaves if i >= half else stays, pl.ds(i % half * rows, rows)) for i, j in enumerate(order)
    }
    choose(place, pieces, targets)


def halve_kernel(follows, mine, other, stays, leaves):
    rows = stays.shape[0]
    stays[...] = mine[pl.ds(0, rows), :] + other[pl.ds(0, rows), :]
    leaves[...] = mine[pl.ds(rows, rows), :] + other[pl.ds(rows, rows), :]


def prefix_kernel(steps, place, follows, *refs):
    parts, moments, refs = refs[:steps], refs[steps : steps + 2], refs[steps + 2 :]
    final, returned = refs[0], refs[1:]
    pair = place[1]
    rows = final.shape[0]
    states = [part[pl.ds(0, rows), :] for part in parts]
    total = states[0]
    for k in range(1, steps):
        total = total + states[k]
    final[...] = total
    for k in range(steps):
        before = jnp.zeros_like(total)
        for m in range(steps):
            before = before + jnp.where((pair ^ m) < (pair ^ k), states[m], 0.0)
        returned[k][pl.ds(0, rows), :] = before
    reply_moment = moments[0][...] + moments[1][...]
    later = [part[pl.ds(rows, rows), :] for part in parts]
    for k in range(steps):
        after = reply_moment
        for m in range(steps):
            after = after + jnp.where((pair ^ m) > (pair ^ k), later[m], 0.0)
        returned[k][pl.ds(rows, rows), :] = after


def halves_kernel(steps, place, follows, kept, received, *refs):
    pieces, finals, refs = refs[:steps], refs[steps : 2 * steps], refs[2 * steps :]
    mine, to_other = refs[:2]
    rows = finals[0].shape[0]
    choose(place, finals, {j: (ref, pl.ds(0, rows)) for j, ref in enumerate(refs[2:])})
    member, pair = place[0], place[1]
    half_rows = kept.shape[0] // 2
    piece_rows = half_rows // steps
    first = member == 0
    for k in range(steps):
        start = pl.multiple_of((pair ^ k) * piece_rows, piece_rows)
        for part in range(2):
            rows = pl.ds(part * half_rows + start, piece_rows)
            sums = pieces[k][pl.ds(part * piece_rows, piece_rows), :]
            add_other = first if part else jnp.logical_not(first)
            mine[rows, :] = sums + jnp.where(add_other, received[rows, :], 0.0)
            to_other[rows, :] = sums + jnp.where(add_other, 0.0, kept[rows, :])


def local_terms(first_head, first_row, query, key, value, cotangent, outs, work):
    inner, query_part, key_part, value_part = outs
    weights, mixing, grad_mixing = work
    heads, rows, size = inner.shape
    block = weights.shape[1]
    count = rows // block
    spans = [pl.ds(i * block, block) for i in range(count)]
    for i in range(count):
        weights[i], weights[count + i] = causal_weights(first_row + i * block, block, size)

    def mix(own):
        h, slot = first_head + own, own % 2
        for i in range(count):
            for j in range(i + 1):
                factor = weights[i if i == j else count + i]
                scores = dot(query[h, spans[i]], key[h, spans[j]], LAST_LAST)
                mixing[slot, spans[i], spans[j]] = (scores * factor).astype(BF16)
                scores = dot(cotangent[h, spans[i]], value[h, spans[j]], LAST_LAST)
                grad_mixing[slot, spans[i], spans[j]] = (scores * factor).astype(BF16)

    mix(0)
    for own in range(heads):
        if own + 1 < heads:
            mix(own + 1)
        h, slot = first_head + own, own % 2
        for i in range(count):
            seen = pl.ds(0, (i + 1) * block)
            inner[own, spans[i]] = dot(mixing[slot, spans[i], seen], value[h, seen], LAST_ROWS)
            query_part[own, spans[i]] = dot(
                grad_mixing[slot, spans[i], seen], key[h, seen], LAST_ROWS
            )
            later = pl.ds(i * block, rows - i * block)
            part = dot(grad_mixing[slot, later, spans[i]], query[h, later], ROWS_ROWS)
            key_part[own, spans[i]] = part.astype(key_part.dtype)
            part = dot(mixing[slot, later, spans[i]], cotangent[h, later], ROWS_ROWS)
            value_part[own, spans[i]] = part.astype(value_part.dtype)


def prompt_local_kernel(place, query, key, value, cotangent, reply_key, reply_value, *refs):
    outs, (r_key, r_value, token), work = refs[1:5], refs[5:8], refs[8:11]
    key_buffer, value_buffer, arrived = refs[11:]
    copies = load((reply_key, reply_value), (key_buffer, value_buffer), arrived)
    local_terms(0, place[2], query, key, value, cotangent, outs, work)
    copies[0].wait()
    r_key[...] = by_head(key_buffer[...])
    copies[1].wait()
    r_value[...] = by_head(value_buffer[...])
    token[...] = jnp.zeros_like(token)


def reply_local_kernel(first_head, place, query, key, value, cotangent, follows, *refs):
    outs, token, work = refs[:4], refs[4], refs[5:]
    local_terms(first_head, place[3], query, key, value, cotangent, outs, work)
    token[...] = jnp.zeros_like(token)


def reply_grads_kernel(follows, key_first, value_first, key_second, value_second, *refs):
    grads, token, staged, left = refs[:2], refs[2], refs[3], refs[4]
    token[...] = jnp.zeros_like(token)
    copies = []
    for i, parts in enumerate(((key_first, key_second), (value_first, value_second))):
        staged[i] = by_head(jnp.concatenate([part[...] for part in parts], 0))
        copies.append(pltpu.make_async_copy(staged.at[i], grads[i], left.at[i]))
        copies[-1].start()
    for copy in copies:
        copy.wait()


def causal_weights(first_row, row_total, head_size):
    rows = lax.broadcasted_iota(jnp.int32, (row_total, row_total), 0)
    columns = lax.broadcasted_iota(jnp.int32, (row_total, row_total), 1)
    scale = lax.rsqrt(float(head_size) * ((rows + first_row).astype(F32) + 1.0))
    return jnp.where(rows >= columns, scale, 0.0), scale


def prompt_final_kernel(place, mine, other, *refs):
    parts, (query, key, value, cotangent), grads = refs[:4], refs[4:8], refs[8:12]
    token, before, after, held, staged, left = refs[12:]
    token[...] = jnp.zeros_like(token)
    member, first_row = place[0], place[2]
    heads, rows, size = query.shape
    half = heads // 2
    scale = row_scale(first_row, rows, size)
    copies = []

    def leave(source, target):
        copies.append(pltpu.make_async_copy(source, target, left.at[len(copies)]))
        copies[-1].start()

    for target, offset in ((before, 0), (after, half)):
        for source, base in ((mine, member * half), (other, (1 - member) * half)):
            for j in range(half):
                target[base + j] = source[pl.ds((offset + j) * size, size), :].astype(BF16)
    for i, (array, state, dims) in enumerate(
        (
            (query, before, LAST_ROWS),
            (cotangent, before, LAST_LAST),
            (value, after, LAST_LAST),
            (key, after, LAST_ROWS),
        )
    ):
        for h in range(heads):
            part = dot(array[h], state[h], dims)
            part = scale * part if i < 2 else part
            held[i, h] = (parts[i][h] + part).astype(BF16)
        staged[i] = by_head(held[i])
        leave(staged.at[i], grads[i])
    for copy in copies:
        copy.wait()


def reply_final_kernel(steps, place, follows, *refs):
    pieces, refs = refs[steps - 1 :: -1], refs[steps:]
    inner, query_part, (query, cotangent, output, query_grad) = refs[:2], refs[2:4], refs[4:8]
    state, held, staged, left = refs[8:]
    half = inner[0].shape[0]
    pair, first_row, length = place[1], place[3], place[4]
    heads, rows, size = query.shape
    piece_rows = pieces[0].shape[0]
    for k in range(steps):
        start = pl.multiple_of((pair ^ k) * piece_rows, piece_rows)
        state[pl.ds(start, piece_rows), :] = pieces[k][...].astype(BF16)
    scale = row_scale(first_row, rows, size)
    live = lax.broadcasted_iota(jnp.int32, (rows, size), 0) < length
    copies = []

    def finish(i, target):
        part = rows // 4
        for start in range(0, rows, part):
            span = pl.ds(start, part)
            staged[i, span] = by_head(held[i, :, span])
            copies.append(
                pltpu.make_async_copy(staged.at[i, span], target.at[span], left.at[len(copies)])
            )
            copies[-1].start()

    for h in range(heads):
        final = state[pl.ds(h * size, size), :]
        whole = inner[h // half][h % half] + scale * dot(query[h], final, LAST_ROWS)
        held[0, h] = jnp.where(live, whole, 0.0).astype(BF16)
    finish(0, output)
    for h in range(heads):
        final = state[pl.ds(h * size, size), :]
        part = scale * dot(cotangent[h], final, LAST_LAST)
        held[1, h] = (query_part[h // half][h % half] + part).astype(BF16)
    finish(1, query_grad)
    for copy in copies:
        copy.wait()


VMEM = pl.BlockSpec(memory_space=pltpu.VMEM)
HBM = pl.BlockSpec(memory_space=pltpu.HBM)
ANY = pl.BlockSpec(memory_space=pl.ANY)


def call(kernel, scalars, arrays, outs, scratch, name):
    arrays = [
        (spec, pltpu.with_memory_space_constraint(array, pltpu.HBM) if spec is HBM else array)
        for spec, array in arrays
    ]
    return pl.pallas_call(
        kernel,
        out_shape=[out for _, out in outs],
        in_specs=[pl.BlockSpec(memory_space=pltpu.SMEM)] * len(scalars) + [s for s, _ in arrays],
        out_specs=[spec for spec, _ in outs],
        scratch_shapes=scratch,
        compiler_params=pltpu.CompilerParams(vmem_limit_bytes=24 << 20),
        cost_estimate=pl.CostEstimate(flops=1, bytes_accessed=1, transcendentals=0),
        name=name,
    )(*scalars, *[array for _, array in arrays])


def held_in(spec, arrays):
    return [(spec, array) for array in arrays]


def shards(
    prompt_query,
    prompt_key,
    prompt_value,
    prompt_cotangent,
    reply_query,
    reply_key,
    reply_value,
    reply_cotangent,
    reply_weight,
    reply_length,
):
    rows, heads, size = prompt_query.shape
    reply_query, reply_key = reply_query[0], reply_key[0]
    reply_value, reply_cotangent = reply_value[0], reply_cotangent[0]
    reply_rows, reply_heads = reply_query.shape[:2]
    block_count = lax.axis_size(PLANE)
    steps = lax.axis_size("resp")
    assert block_count == 2 * steps and steps & (steps - 1) == 0
    block_index = lax.axis_index(PLANE)
    resp_index = lax.axis_index("resp")
    pair_index, member = block_index // 2, block_index % 2
    half_rows = heads // 2 * size
    piece_rows = half_rows // steps
    place = jnp.stack(
        [
            member,
            pair_index,
            block_index * rows,
            block_count * rows,
            reply_length[0],
            resp_index,
        ]
    ).astype(jnp.int32)
    shape = jax.ShapeDtypeStruct
    prompt_bf16 = shape((rows, heads, size), BF16)
    reply_bf16 = shape((reply_rows, reply_heads, size), BF16)
    prompt_held = shape((heads, rows, size), BF16)
    reply_held = shape((reply_heads, reply_rows, size), BF16)
    piece = shape((piece_rows, size), F32)
    two_pieces = shape((2 * piece_rows, size), F32)
    two_halves = shape((2 * half_rows, size), F32)

    def scratch(held, count=None):
        return pltpu.VMEM(held.shape if count is None else (count, *held.shape), held.dtype)

    sent, kept, key, value, query, cotangent, r_query, r_cotangent, *moments = call(
        functools.partial(moments_kernel, steps),
        [place, reply_weight],
        held_in(
            HBM,
            [prompt_key, prompt_value, prompt_query, prompt_cotangent, reply_query, reply_cotangent],
        ),
        held_in(
            VMEM, [two_halves] * 2 + [prompt_held] * 4 + [reply_held] * 2 + [piece] * steps
        ),
        [scratch(prompt_bf16)] * 4
        + [scratch(reply_bf16)] * 2
        + [scratch(prompt_held), scratch(reply_held)]
        + [pltpu.VMEM((reply_heads * size, size), F32)]
        + [pltpu.SemaphoreType.DMA((6,))],
        "moments",
    )
    received = pair_step(sent)
    moments = plane_exchange(moments)
    pieces = call(
        functools.partial(pair_kernel, steps),
        [place],
        held_in(VMEM, [kept, received]),
        held_in(VMEM, [two_pieces] * steps),
        [],
        "pair_sums",
    )
    parts = plane_exchange(pieces)
    half_heads = reply_heads // 2
    half_reply = shape((half_heads, reply_rows, size), F32)
    half_held = shape((half_heads, reply_rows, size), BF16)
    prompt_wide = shape((heads, rows, size), F32)
    token = shape((8, 128), F32)

    def work(total):
        block = min(BLOCK, total)
        mixing = pltpu.VMEM((2, total, total), BF16)
        return [pltpu.VMEM((2 * (total // block), block, block), F32), mixing, mixing]

    prompt_arrays = held_in(VMEM, [query, key, value, cotangent])
    *prompt_parts, r_key, r_value, done = call(
        prompt_local_kernel,
        [place],
        prompt_arrays + held_in(HBM, [reply_key, reply_value]) + held_in(ANY, pieces[:1]),
        held_in(VMEM, [prompt_wide] * 4 + [reply_held] * 2 + [token]),
        work(rows) + [scratch(reply_bf16)] * 2 + [pltpu.SemaphoreType.DMA((2,))],
        "prompt_local",
    )
    stays, leaves, done = call(
        functools.partial(choose_kernel, steps),
        [place],
        held_in(ANY, [done]) + held_in(VMEM, moments),
        held_in(VMEM, [shape((steps // 2 * piece_rows, size), F32)] * 2 + [token]),
        [],
        "choose_moments",
    )
    reply_arrays = held_in(VMEM, [r_query, r_key, r_value, r_cotangent])
    reply_terms = held_in(VMEM, [half_reply] * 2 + [half_held] * 2 + [token])
    inner_first, part_first, key_first, value_first, done = call(
        functools.partial(reply_local_kernel, 0),
        [place],
        reply_arrays + held_in(ANY, [done]),
        reply_terms,
        work(reply_rows),
        "reply_local_first",
    )
    masks = resp_masks(steps)
    for mask in masks[:-1]:
        rows_left = stays.shape[0] // 2
        stays, leaves = call(
            halve_kernel,
            [],
            held_in(ANY, [done]) + held_in(VMEM, [stays, resp_step(leaves, mask)]),
            held_in(VMEM, [shape((rows_left, size), F32)] * 2),
            [],
            "reply_moments",
        )
    inner_second, part_second, key_second, value_second, done = call(
        functools.partial(reply_local_kernel, half_heads),
        [place],
        reply_arrays + held_in(ANY, [leaves]),
        reply_terms,
        work(reply_rows),
        "reply_local_second",
    )
    final, *returned = call(
        functools.partial(prefix_kernel, steps),
        [place],
        held_in(ANY, [done]) + held_in(VMEM, [*parts, stays, resp_step(leaves, masks[-1])]),
        held_in(VMEM, [piece] + [two_pieces] * steps),
        [],
        "prefix_sums",
    )
    finals = resp_gather(final)
    returned = plane_exchange(returned)
    reply_dkey, reply_dvalue, done = call(
        reply_grads_kernel,
        [],
        held_in(ANY, [final])
        + held_in(VMEM, [key_first, value_first, key_second, value_second]),
        held_in(HBM, [reply_bf16] * 2) + held_in(VMEM, [token]),
        [scratch(reply_bf16, 2), pltpu.SemaphoreType.DMA((2,))],
        "reply_grads",
    )
    mine, to_other, *finals = call(
        functools.partial(halves_kernel, steps),
        [place],
        held_in(ANY, [done]) + held_in(VMEM, [kept, received, *returned, *finals]),
        held_in(VMEM, [two_halves] * 2 + [piece] * steps),
        [],
        "halves",
    )
    finals = plane_exchange(finals)
    other = pair_step(to_other)
    *prompt_results, done = call(
        prompt_final_kernel,
        [place],
        held_in(VMEM, [mine, other, *prompt_parts]) + prompt_arrays,
        held_in(HBM, [prompt_bf16] * 4) + held_in(VMEM, [token]),
        [pltpu.VMEM((heads, size, size), BF16)] * 2
        + [scratch(prompt_held, 4), scratch(prompt_bf16, 4)]
        + [pltpu.SemaphoreType.DMA((4,))],
        "prompt_final",
    )
    prompt_output, prompt_dquery, prompt_dkey, prompt_dvalue = prompt_results
    reply_output, reply_dquery = call(
        functools.partial(reply_final_kernel, steps),
        [place],
        held_in(ANY, [done])
        + held_in(VMEM, [*finals[::-1], inner_first, inner_second, part_first, part_second])
        + held_in(VMEM, [r_query, r_cotangent]),
        held_in(HBM, [reply_bf16] * 2),
        [
            pltpu.VMEM((reply_heads * size, size), BF16),
            scratch(reply_held, 2),
            scratch(reply_bf16, 2),
            pltpu.SemaphoreType.DMA((8,)),
        ],
        "reply_final",
    )
    return (
        prompt_output,
        reply_output[None],
        prompt_dquery,
        prompt_dkey,
        prompt_dvalue,
        reply_dquery[None],
        reply_dkey[None],
        reply_dvalue[None],
    )


def solution(mesh):
    prompt = P(PLANE, "resp", None)
    reply = P("resp", None, PLANE, None)
    return jax.shard_map(
        shards,
        mesh=mesh,
        in_specs=(prompt,) * 4 + (reply,) * 4 + (P("resp"),) * 2,
        out_specs=(prompt, reply, prompt, prompt, prompt, reply, reply, reply),
        check_vma=False,
    )
```
